32 devices in a mesh: graph: 8 (over z, x), feat: 4 (over y, core).
Axes of the slice: x: 2, y: 2, z: 4, core: 2. Of those that a mesh axis runs over, the one named last changes fastest.
Arguments:
- features: bfloat16 [128, 65536], P('feat', 'graph'), may hold values from -6 to 6
- w_self: bfloat16 [128, 128], replicated, may hold values from -0.5 to 0.5
- w_neigh: bfloat16 [128, 128], replicated, may hold values from -0.5 to 0.5
- bias: float32 [128], replicated, may hold values from -3 to 3
- hub_pick: int32 [16], P('graph'), may hold values from 0 to 63
- halo_send: int32 [128], P('graph'), may hold values from 0 to 63
- tile_dst: int32 [2048], P('graph'), may hold values from 0 to 63
- tile_src: int32 [2048], P('graph'), may hold values from 0 to 95, as said below
- tile_edges: int32 [2048], P('graph'), may hold values from 1 to 128, as said below
- tile_count: int32 [8], P('graph'), may hold values from 64 to 256, as said below
- edge_src: int32 [2048, 128], P('graph'), may hold values from 0 to 127
- edge_dst: int32 [2048, 128], P('graph'), may hold values from 0 to 127
Outputs:
- updated: bfloat16 [128, 65536], P('feat', 'graph')
The draws below stay inside these ranges and needn't reach their ends.
Inputs may be any that keep to these rules, and one draw needn't show every extreme that they name: `tile_src`: A tile's source index counts into table_p: below 64 own blocks, then 16 hub blocks, then 2 * 8 halo blocks; the largest value occurs in every draw. `tile_edges`: some tile of every draw has all 128 slots live. `tile_count`: some partition of every draw has all 256 tiles live.
All inputs are finite; a program needn't handle non-finite values.
Results may differ from the reference program's by a relative error of at most 0.0015.
Values may be sent and summed in bfloat16 or wider, within the bound.
A program may use at most 64 MiB of HBM per device.

```python
import jax
import jax.numpy as jnp
from jax import lax

F = 128
BLOCK = 128
EDGES = 128
NB_DEV = 64
HUB_DEV = 2
HALO = 8
TILES_DEV = 256
HUBS = 16
SLOTS = 96
NODES = 65536
N_GRAPH = 8


def draw_tile_src(key, part):
    key = jax.random.fold_in(key, 11)
    kinds, local_key, hub_key, halo_key, spot_key = jax.random.split(key, 5)
    total = N_GRAPH * TILES_DEV
    category = jax.random.randint(kinds, (total,), 0, 4)
    local_slot = jax.random.randint(local_key, (total,), 0, NB_DEV)
    hub_slot = NB_DEV + jax.random.randint(hub_key, (total,), 0, HUBS)
    halo_slot = NB_DEV + HUBS + jax.random.randint(halo_key, (total,), 0, 2 * HALO)
    slots = jnp.where(category < 2, local_slot, jnp.where(category == 2, hub_slot, halo_slot))
    spot = jax.random.randint(spot_key, (), 0, total)
    return slots.at[spot].set(SLOTS - 1).astype(jnp.int32)


def draw_tile_edges(key, part):
    key = jax.random.fold_in(key, 23)
    count_key, spot_key = jax.random.split(key)
    total = N_GRAPH * TILES_DEV
    counts = jax.random.randint(count_key, (total,), 1, EDGES + 1)
    spot = jax.random.randint(spot_key, (), 0, total)
    return counts.at[spot].set(EDGES).astype(jnp.int32)


def draw_tile_count(key, part):
    key = jax.random.fold_in(key, 37)
    count_key, spot_key = jax.random.split(key)
    counts = jax.random.randint(count_key, (N_GRAPH,), TILES_DEV // 4, TILES_DEV + 1)
    spot = jax.random.randint(spot_key, (), 0, N_GRAPH)
    return counts.at[spot].set(TILES_DEV).astype(jnp.int32)


def set_ends(drawn, own_key, low, high):
    longest = drawn.shape.index(max(drawn.shape))
    spots = []
    for shift in (0, 1):
        where = [jax.random.randint(jax.random.fold_in(own_key, axis), (), 0, length) for axis, length in enumerate(drawn.shape)]
        where[longest] = (where[longest] + shift) % drawn.shape[longest]
        spots.append(tuple(where))
    return drawn.at[spots[0]].set(low).at[spots[1]].set(high)


def level_of(rng, dims, shards, smallest, high):
    gain = 1.0
    for axis_at, parts in shards:
        heights = jax.random.uniform(jax.random.fold_in(jax.random.fold_in(rng, 6), axis_at), (parts,), jnp.float32, smallest / len(shards), high / len(shards))
        gain = gain * jnp.repeat(jnp.exp(heights), dims[axis_at] // parts).reshape((-1,) + (1,) * (len(dims) - 1 - axis_at))
    return gain


def noise(stream_key, extent, width, most, shards=(), kind=jnp.bfloat16):
    loudness = level_of(stream_key, extent, shards, -0.22, 0.18) if shards else 1.0
    array = jax.random.normal(stream_key, extent, jnp.float32) * width * loudness
    return jnp.minimum(jnp.maximum(array, -most), most).astype(kind)


def setup_inputs(seed: int = 0) -> dict:
    keys = jax.random.split(jax.random.key(seed), 13)
    features = noise(keys[0], (F, NODES), 1.0, 6.0, ((0, 4), (1, 8)))
    w_self = noise(keys[1], (F, F), F ** -0.5, 0.5)
    w_neigh = noise(keys[2], (F, F), F ** -0.5, 0.5)
    bias = noise(keys[3], (F,), 0.5, 3.0, (), jnp.float32)
    hub_pick = set_ends(jax.random.randint(keys[4], (HUBS,), 0, NB_DEV), jax.random.fold_in(keys[4], 1), 0, NB_DEV - 1).astype(jnp.int32)
    halo_send = set_ends(jax.random.randint(keys[5], (N_GRAPH * 2 * HALO,), 0, NB_DEV), jax.random.fold_in(keys[5], 1), 0, NB_DEV - 1).astype(jnp.int32)
    tile_dst = set_ends(jax.random.randint(keys[6], (N_GRAPH * TILES_DEV,), 0, NB_DEV), jax.random.fold_in(keys[6], 1), 0, NB_DEV - 1).astype(jnp.int32)
    tile_src = draw_tile_src(jax.random.fold_in(keys[12], 71), 0)
    tile_edges = draw_tile_edges(jax.random.fold_in(keys[12], 71), 0)
    tile_count = draw_tile_count(jax.random.fold_in(keys[12], 71), 0)
    edge_src = set_ends(jax.random.randint(keys[10], (N_GRAPH * TILES_DEV, EDGES), 0, BLOCK), jax.random.fold_in(keys[10], 1), 0, BLOCK - 1).astype(jnp.int32)
    edge_dst = set_ends(jax.random.randint(keys[11], (N_GRAPH * TILES_DEV, EDGES), 0, BLOCK), jax.random.fold_in(keys[11], 1), 0, BLOCK - 1).astype(jnp.int32)
    return dict(features=features, w_self=w_self, w_neigh=w_neigh, bias=bias, hub_pick=hub_pick, halo_send=halo_send, tile_dst=tile_dst, tile_src=tile_src, tile_edges=tile_edges, tile_count=tile_count, edge_src=edge_src, edge_dst=edge_dst)


def partition_mean(blocks, hub_rows, halo_send, tile_dst, tile_src, tile_edges, tile_count, edge_src, edge_dst, partition):
    previous = (partition - 1) % N_GRAPH
    following = (partition + 1) % N_GRAPH
    left_list = lax.dynamic_slice_in_dim(halo_send, (previous * 2 * HALO + HALO).astype(jnp.int32), HALO)
    right_list = lax.dynamic_slice_in_dim(halo_send, (following * 2 * HALO).astype(jnp.int32), HALO)
    own_blocks = blocks[:, partition]
    left_rows = blocks[:, previous][:, left_list]
    right_rows = blocks[:, following][:, right_list]
    table = jnp.concatenate([own_blocks, hub_rows, left_rows, right_rows], axis=1).reshape(F, SLOTS * BLOCK)
    first_tile = (partition * TILES_DEV).astype(jnp.int32)
    dst_part = lax.dynamic_slice_in_dim(tile_dst, first_tile, TILES_DEV)
    src_part = lax.dynamic_slice_in_dim(tile_src, first_tile, TILES_DEV)
    edges_part = lax.dynamic_slice_in_dim(tile_edges, first_tile, TILES_DEV)
    esrc_part = lax.dynamic_slice_in_dim(edge_src, first_tile, TILES_DEV, 0)
    edst_part = lax.dynamic_slice_in_dim(edge_dst, first_tile, TILES_DEV, 0)
    source = (src_part[:, None] * BLOCK + esrc_part).reshape(-1)
    target = (dst_part[:, None] * BLOCK + edst_part).reshape(-1)
    live = (jnp.arange(EDGES, dtype=jnp.int32)[None, :] < edges_part[:, None]) & (jnp.arange(TILES_DEV, dtype=jnp.int32)[:, None] < tile_count[partition])
    live = live.reshape(-1)
    values = jnp.where(live[None, :], table[:, source].astype(jnp.float32), jnp.float32(0.0))
    sums = jnp.zeros((F, NB_DEV * BLOCK), jnp.float32).at[:, target].add(values)
    degree = jnp.zeros((NB_DEV * BLOCK,), jnp.float32).at[target].add(live.astype(jnp.float32))
    return (sums / jnp.maximum(degree, 1.0)[None, :]).astype(jnp.bfloat16)


def reference(features, w_self, w_neigh, bias, hub_pick, halo_send, tile_dst, tile_src, tile_edges, tile_count, edge_src, edge_dst):
    blocks = features.reshape(F, N_GRAPH, NB_DEV, BLOCK)
    owners = (jnp.arange(HUBS, dtype=jnp.int32) // HUB_DEV).astype(jnp.int32)
    hub_rows = blocks[:, owners, hub_pick]

    def one_partition(partition):
        return partition_mean(blocks, hub_rows, halo_send, tile_dst, tile_src, tile_edges, tile_count, edge_src, edge_dst, partition)

    means = lax.map(one_partition, jnp.arange(N_GRAPH, dtype=jnp.int32))
    mean = jnp.transpose(means, (1, 0, 2)).reshape(F, NODES)
    total = jnp.dot(w_self, features, preferred_element_type=jnp.float32) + jnp.dot(w_neigh, mean, preferred_element_type=jnp.float32)
    return jax.nn.relu(total + bias[:, None]).astype(jnp.bfloat16)
```

```python
import functools

import jax
import jax.numpy as jnp
from jax import lax
from jax.experimental import pallas as pl
from jax.experimental.pallas import tpu as pltpu
from jax.sharding import PartitionSpec as P

BLOCK = 128
GROUP = 8
MESH = pl.DeviceIdType.MESH


def block_at(index):
    return pl.ds(pl.multiple_of(index * BLOCK, BLOCK), BLOCK)


def exchange_kernel(
    n,
    hub_per,
    halo,
    feat_ref,
    pick_ref,
    send_ref,
    ext_ref,
    own_blocks,
    hub_buf,
    halo_buf,
    send_sem,
    recv_sem,
):
    me = lax.axis_index("graph")
    col = lax.axis_index("feat")
    barrier = pltpu.get_barrier_semaphore()
    for k in range(1, n):
        pl.semaphore_signal(
            barrier, inc=1, device_id=(lax.rem(me + k, n), col), device_id_type=MESH
        )
    for b in range(own_blocks.shape[0]):
        own_blocks[b] = feat_ref[:, b * BLOCK : (b + 1) * BLOCK]
    for j in range(hub_per):
        hub_buf[:, j * BLOCK : (j + 1) * BLOCK] = own_blocks[pick_ref[j]]
    for j in range(2 * halo):
        halo_buf[:, j * BLOCK : (j + 1) * BLOCK] = own_blocks[send_ref[j]]
    hub_cols = hub_per * BLOCK
    halo_cols = halo * BLOCK
    own = pl.ds(pl.multiple_of(me * hub_cols, BLOCK), hub_cols)
    pl.semaphore_wait(barrier, n - 1)
    copies = []
    for side, peer in ((0, lax.rem(me + n - 1, n)), (1, lax.rem(me + 1, n))):
        start = n * hub_cols + (1 - side) * halo_cols
        copies.append(
            pltpu.make_async_remote_copy(
                src_ref=halo_buf.at[:, pl.ds(side * halo_cols, halo_cols)],
                dst_ref=ext_ref.at[:, pl.ds(start, halo_cols)],
                send_sem=send_sem.at[n + side],
                recv_sem=recv_sem.at[n + side],
                device_id=(peer, col),
                device_id_type=MESH,
            )
        )
    for k in range(1, n):
        copies.append(
            pltpu.make_async_remote_copy(
                src_ref=hub_buf,
                dst_ref=ext_ref.at[:, own],
                send_sem=send_sem.at[k],
                recv_sem=recv_sem.at[k],
                device_id=(lax.rem(me + k, n), col),
                device_id_type=MESH,
            )
        )
    for copy in copies:
        copy.start()
    ext_ref[:, own] = hub_buf[...]
    for copy in copies:
        copy.wait()


def exchange(features, hub_pick, halo_send, n):
    rows = features.shape[0]
    hub_per = hub_pick.shape[0]
    halo = halo_send.shape[0] // 2
    width = (n * hub_per + 2 * halo) * BLOCK
    vmem = pl.BlockSpec(memory_space=pltpu.VMEM)
    smem = pl.BlockSpec(memory_space=pltpu.SMEM)
    return pl.pallas_call(
        functools.partial(exchange_kernel, n, hub_per, halo),
        out_shape=jax.ShapeDtypeStruct((rows, width), jnp.bfloat16),
        in_specs=[vmem, smem, smem],
        out_specs=vmem,
        scratch_shapes=[
            pltpu.VMEM((features.shape[1] // BLOCK, rows, BLOCK), jnp.bfloat16),
            pltpu.VMEM((rows, hub_per * BLOCK), jnp.bfloat16),
            pltpu.VMEM((rows, 2 * halo * BLOCK), jnp.bfloat16),
            pltpu.SemaphoreType.DMA((n + 2,)),
            pltpu.SemaphoreType.DMA((n + 2,)),
        ],
        compiler_params=pltpu.CompilerParams(
            collective_id=0, has_side_effects=True, vmem_limit_bytes=32 * 1024 * 1024
        ),
    )(features, hub_pick, halo_send)


def aggregate_kernel(
    feat_ref,
    ext_ref,
    dst_ref,
    src_ref,
    edges_ref,
    count_ref,
    esrc_ref,
    edst_ref,
    mean_ref,
    table,
    sums,
):
    rows, nodes = feat_ref.shape
    blocks = nodes // BLOCK
    extra = ext_ref.shape[1] // BLOCK

    def unpack_own(b, carry):
        table[b] = feat_ref[:, block_at(b)].astype(jnp.float32)
        sums[b] = jnp.zeros_like(sums[b])
        return carry

    def unpack_ext(b, carry):
        table[blocks + b] = ext_ref[:, block_at(b)].astype(jnp.float32)
        return carry

    lax.fori_loop(0, blocks, unpack_own, 0, unroll=4)
    lax.fori_loop(0, extra, unpack_ext, 0, unroll=4)
    count = count_ref[0]
    lane = lax.broadcasted_iota(jnp.int32, (1, BLOCK), 1)
    node = lax.broadcasted_iota(jnp.int32, (BLOCK, BLOCK), 0)
    ones = jnp.ones((16, BLOCK), jnp.bfloat16)

    def group(g, carry):
        first = g * GROUP
        esrc = esrc_ref[pl.ds(pl.multiple_of(first, GROUP), GROUP), :]
        edst = edst_ref[pl.ds(pl.multiple_of(first, GROUP), GROUP), :]
        parts = []
        for j in range(GROUP):
            t = first + j
            live = jnp.where(t < count, edges_ref[t], 0)
            target = jnp.where(lane < live, edst[j : j + 1, :], -1)
            values = table[src_ref[t]]
            index = jnp.broadcast_to(esrc[j : j + 1, :], values.shape)
            picked = jnp.take_along_axis(values, index, axis=1, mode="promise_in_bounds")
            left = jnp.concatenate([picked.astype(jnp.bfloat16), ones], axis=0)
            hot = jnp.where(node == target, 1.0, 0.0).astype(jnp.bfloat16)
            parts.append(
                lax.dot_general(
                    left, hot, (((1,), (1,)), ((), ())), preferred_element_type=jnp.float32
                )
            )
        for j in range(GROUP):
            sums[dst_ref[first + j]] += parts[j]
        return carry

    lax.fori_loop(0, (count + GROUP - 1) // GROUP, group, 0)

    def finish(b, carry):
        total = sums[b]
        degree = jnp.maximum(total[rows : rows + 1, :], 1.0)
        mean_ref[:, block_at(b)] = (total[:rows, :] / degree).astype(jnp.bfloat16)
        return carry

    lax.fori_loop(0, blocks, finish, 0, unroll=4)


def aggregate(features, ext, tile_dst, tile_src, tile_edges, tile_count, edge_src, edge_dst):
    rows, nodes = features.shape
    blocks = nodes // BLOCK
    slots = blocks + ext.shape[1] // BLOCK
    vmem = pl.BlockSpec(memory_space=pltpu.VMEM)
    smem = pl.BlockSpec(memory_space=pltpu.SMEM)
    return pl.pallas_call(
        aggregate_kernel,
        out_shape=jax.ShapeDtypeStruct((rows, nodes), jnp.bfloat16),
        in_specs=[vmem, vmem, smem, smem, smem, smem, vmem, vmem],
        out_specs=vmem,
        scratch_shapes=[
            pltpu.VMEM((slots, rows, BLOCK), jnp.float32),
            pltpu.VMEM((blocks, rows + 16, BLOCK), jnp.float32),
        ],
        compiler_params=pltpu.CompilerParams(vmem_limit_bytes=32 * 1024 * 1024),
    )(features, ext, tile_dst, tile_src, tile_edges, tile_count, edge_src, edge_dst)


def shards(
    n,
    features,
    w_self,
    w_neigh,
    bias,
    hub_pick,
    halo_send,
    tile_dst,
    tile_src,
    tile_edges,
    tile_count,
    edge_src,
    edge_dst,
):
    feat_rows = features.shape[0]
    input_piece = lax.all_gather(features, "feat", axis=0, tiled=True)
    ext = exchange(features, hub_pick, halo_send, n)
    own_means = aggregate(
        features, ext, tile_dst, tile_src, tile_edges, tile_count, edge_src, edge_dst
    )
    feat_start = lax.axis_index("feat") * feat_rows
    self_rows = lax.dynamic_slice_in_dim(w_self, feat_start, feat_rows, 0)
    neigh_rows = lax.dynamic_slice_in_dim(w_neigh, feat_start, feat_rows, 0)
    mean_piece = lax.all_gather(own_means, "feat", axis=0, tiled=True)
    total = jnp.dot(self_rows, input_piece, preferred_element_type=jnp.float32) + jnp.dot(
        neigh_rows, mean_piece, preferred_element_type=jnp.float32
    )
    bias_rows = lax.dynamic_slice_in_dim(bias, feat_start, feat_rows, 0)
    return jax.nn.relu(total + bias_rows[:, None]).astype(jnp.bfloat16)


def solution(mesh):
    in_specs = (
        P("feat", "graph"),
        P(),
        P(),
        P(),
        P("graph"),
        P("graph"),
        P("graph"),
        P("graph"),
        P("graph"),
        P("graph"),
        P("graph", None),
        P("graph", None),
    )
    return jax.shard_map(
        functools.partial(shards, mesh.shape["graph"]),
        mesh=mesh,
        in_specs=in_specs,
        out_specs=P("feat", "graph"),
        check_vma=False,
    )
```

```python
import functools

import jax
import jax.numpy as jnp
from jax import lax
from jax.experimental import pallas as pl
from jax.experimental.pallas import tpu as pltpu
from jax.sharding import PartitionSpec as P

BLOCK = 128
GROUP = 8
CHUNKS = 2
MESH = pl.DeviceIdType.MESH


def block_at(index):
    return pl.ds(pl.multiple_of(index * BLOCK, BLOCK), BLOCK)


def layer_kernel(
    n,
    f,
    features,
    w_self,
    w_neigh,
    bias,
    hub_pick,
    halo_send,
    links,
    tile_src,
    tile_edges,
    tile_count,
    edge_src,
    edge_dst,
    out,
    feat,
    weight,
    bias_row,
    pick,
    send,
    link,
    src,
    edges,
    count_ref,
    esrc,
    edst,
    table,
    hub_buf,
    halo_buf,
    ext,
    running,
    means,
    joined,
    result,
    local_sem,
    send_sem,
    recv_sem,
    feat_send,
    feat_recv,
    mean_send,
    mean_recv,
    out_send,
    out_recv,
    own_sem,
):
    rows, nodes = feat.shape
    blocks = nodes // BLOCK
    total_rows = rows * f
    quarter = nodes // f
    per_quarter = quarter // BLOCK
    tiles = src.shape[0]
    hub_per = pick.shape[0]
    halo = send.shape[0] // 2
    me = lax.axis_index("graph")
    col = lax.axis_index("feat")
    high = col // 2
    low = lax.rem(col, 2)
    half = f // 2
    turns = [(a, b) for a in list(range(1, half)) + [0] for b in (0, 1) if (a, b) != (0, 0)]
    peers = [lax.rem(high + a, half) * 2 + lax.rem(low + b, 2) for a, b in turns]

    pairs = (
        (features, feat),
        (hub_pick, pick),
        (halo_send, send),
        (w_self, weight.at[:, pl.ds(0, total_rows)]),
        (w_neigh, weight.at[:, pl.ds(total_rows, total_rows)]),
        (bias, bias_row),
        (links, link),
        (tile_src, src),
        (tile_edges, edges),
        (tile_count, count_ref),
        (edge_src, esrc),
        (edge_dst, edst),
    )
    loads = [pltpu.make_async_copy(a, b, local_sem.at[i]) for i, (a, b) in enumerate(pairs)]
    for load in loads:
        load.start()
    barrier = pltpu.get_barrier_semaphore()
    for k in range(1, n):
        pl.semaphore_signal(
            barrier, inc=1, device_id=(lax.rem(me + k, n), col), device_id_type=MESH
        )
    for peer in peers:
        pl.semaphore_signal(barrier, inc=1, device_id=(me, peer), device_id_type=MESH)
    running[0] = jnp.zeros_like(running[0])
    for load in loads[:3]:
        load.wait()
    for b in range(blocks):
        table[b] = feat[:, b * BLOCK : (b + 1) * BLOCK].astype(jnp.float32)
    for j in range(2 * halo):
        halo_buf[:, j * BLOCK : (j + 1) * BLOCK] = table[send[j]].astype(jnp.bfloat16)
    for j in range(hub_per):
        hub_buf[:, j * BLOCK : (j + 1) * BLOCK] = table[pick[j]].astype(jnp.bfloat16)
    hub_cols = hub_per * BLOCK
    halo_cols = halo * BLOCK
    own_hubs = pl.ds(pl.multiple_of(me * hub_cols, BLOCK), hub_cols)
    own_rows = pl.ds(pl.multiple_of(col * rows, rows), rows)
    own_nodes = pl.ds(pl.multiple_of(col * quarter, BLOCK), quarter)
    pl.semaphore_wait(barrier, n - 1 + f - 1)

    copies = []
    for side, peer in ((0, lax.rem(me + n - 1, n)), (1, lax.rem(me + 1, n))):
        start = n * hub_cols + (1 - side) * halo_cols
        copies.append(
            pltpu.make_async_remote_copy(
                src_ref=halo_buf.at[:, pl.ds(side * halo_cols, halo_cols)],
                dst_ref=ext.at[:, pl.ds(start, halo_cols)],
                send_sem=send_sem.at[n + side],
                recv_sem=recv_sem.at[n + side],
                device_id=(peer, col),
                device_id_type=MESH,
            )
        )
    for k in range(1, n):
        copies.append(
            pltpu.make_async_remote_copy(
                src_ref=hub_buf,
                dst_ref=ext.at[:, own_hubs],
                send_sem=send_sem.at[k],
                recv_sem=recv_sem.at[k],
                device_id=(lax.rem(me + k, n), col),
                device_id_type=MESH,
            )
        )
    for copy in copies:
        copy.start()
    feat_copies = []
    for k, peer in enumerate(peers):
        feat_copies.append(
            pltpu.make_async_remote_copy(
                src_ref=feat.at[:, pl.ds(pl.multiple_of(peer * quarter, BLOCK), quarter)],
                dst_ref=joined.at[own_rows, :],
                send_sem=feat_send.at[k],
                recv_sem=feat_recv.at[k],
                device_id=(me, peer),
                device_id_type=MESH,
            )
        )
        feat_copies[-1].start()
    joined[own_rows, :] = feat[:, own_nodes]
    ext[:, own_hubs] = hub_buf[...]
    for load in loads[3:]:
        load.wait()
    for copy in copies:
        copy.wait()
    for b in range(ext.shape[1] // BLOCK):
        table[blocks + b] = ext[:, b * BLOCK : (b + 1) * BLOCK].astype(jnp.float32)

    count = count_ref[0]
    lane = lax.broadcasted_iota(jnp.int32, (1, BLOCK), 1)
    node = lax.broadcasted_iota(jnp.int32, (BLOCK, BLOCK), 0).astype(jnp.bfloat16)
    ones = jnp.ones((16, BLOCK), jnp.bfloat16)
    unit = jnp.ones((BLOCK, BLOCK), jnp.bfloat16)
    none = jnp.zeros((BLOCK, BLOCK), jnp.bfloat16)

    def group(g, carry):
        first = pl.multiple_of(g * GROUP, GROUP)
        esrc_rows = esrc[pl.ds(first, GROUP), :]
        edst_rows = edst[pl.ds(first, GROUP), :]
        parts = []
        for j in range(GROUP):
            t = first + j
            live = jnp.where(t < count, edges[t], 0)
            target = jnp.where(lane < live, edst_rows[j : j + 1, :], -1).astype(jnp.bfloat16)
            values = table[src[t]]
            index = jnp.broadcast_to(esrc_rows[j : j + 1, :], values.shape)
            picked = jnp.take_along_axis(values, index, axis=1, mode="promise_in_bounds")
            left = jnp.concatenate([picked.astype(jnp.bfloat16), ones], axis=0)
            hot = jnp.where(node == target, unit, none)
            parts.append(
                lax.dot_general(
                    left, hot, (((1,), (1,)), ((), ())), preferred_element_type=jnp.float32
                )
            )
        for j in range(GROUP):
            running[first + j + 1] = running[link[first + j]] + parts[j]
        return carry

    lax.fori_loop(0, tiles // GROUP, group, 0)

    def quarter_means(owner):
        def finish(i, carry):
            b = owner * per_quarter + i
            total = running[link[tiles + b]]
            degree = jnp.maximum(total[rows : rows + 1, :], 1.0)
            means[:, block_at(b)] = (total[:rows, :] / degree).astype(jnp.bfloat16)
            return carry

        lax.fori_loop(0, per_quarter, finish, 0, unroll=4)

    mean_rows = pl.ds(pl.multiple_of(total_rows + col * rows, rows), rows)
    mean_copies = []
    for k, peer in enumerate(peers):
        quarter_means(peer)
        mean_copies.append(
            pltpu.make_async_remote_copy(
                src_ref=means.at[:, pl.ds(pl.multiple_of(peer * quarter, BLOCK), quarter)],
                dst_ref=joined.at[mean_rows, :],
                send_sem=mean_send.at[k],
                recv_sem=mean_recv.at[k],
                device_id=(me, peer),
                device_id_type=MESH,
            )
        )
        mean_copies[-1].start()
    quarter_means(col)
    joined[mean_rows, :] = means[:, own_nodes]
    column = jnp.transpose(jnp.broadcast_to(bias_row[...], (BLOCK, total_rows)))[:, :1]
    for copy in feat_copies:
        copy.wait()
    for copy in mean_copies:
        copy.wait()
    width = quarter // CHUNKS
    out_copies = []
    own_copies = []
    for c in range(CHUNKS):
        cols = pl.ds(c * width, width)
        total = jnp.dot(weight[...], joined[:, cols], preferred_element_type=jnp.float32)
        result[:, cols] = jnp.maximum(total + column, 0.0).astype(jnp.bfloat16)
        place = pl.ds(pl.multiple_of(col * quarter + c * width, BLOCK), width)
        for k, peer in enumerate(peers):
            out_copies.append(
                pltpu.make_async_remote_copy(
                    src_ref=result.at[pl.ds(pl.multiple_of(peer * rows, rows), rows), cols],
                    dst_ref=out.at[:, place],
                    send_sem=out_send.at[c, k],
                    recv_sem=out_recv.at[c, k],
                    device_id=(me, peer),
                    device_id_type=MESH,
                )
            )
            out_copies[-1].start()
        own_copies.append(
            pltpu.make_async_copy(
                result.at[own_rows, cols], out.at[:, place], own_sem.at[c]
            )
        )
        own_copies[-1].start()
    for copy in out_copies + own_copies:
        copy.wait()


def shards(
    n,
    f,
    features,
    w_self,
    w_neigh,
    bias,
    hub_pick,
    halo_send,
    tile_dst,
    tile_src,
    tile_edges,
    tile_count,
    edge_src,
    edge_dst,
):
    rows, nodes = features.shape
    blocks = nodes // BLOCK
    tiles = tile_dst.shape[0]
    hub_per = hub_pick.shape[0]
    halo = halo_send.shape[0] // 2
    extra = n * hub_per + 2 * halo
    full = rows * f
    quarter = nodes // f
    keys = jnp.concatenate([tile_dst, jnp.arange(blocks, dtype=jnp.int32)])
    order = jnp.arange(tiles, dtype=jnp.int32)
    bound = jnp.minimum(jnp.arange(tiles + blocks, dtype=jnp.int32), tiles)
    earlier = (keys[:, None] == tile_dst[None, :]) & (order[None, :] < bound[:, None])
    links = jnp.max(jnp.where(earlier, order[None, :] + 1, 0), axis=1)
    bf16, f32, i32 = jnp.bfloat16, jnp.float32, jnp.int32
    vmem, smem, dma = pltpu.VMEM, pltpu.SMEM, pltpu.SemaphoreType.DMA
    return pl.pallas_call(
        functools.partial(layer_kernel, n, f),
        out_shape=jax.ShapeDtypeStruct((rows, nodes), bf16),
        in_specs=[pl.BlockSpec(memory_space=pl.ANY)] * 12,
        out_specs=pl.BlockSpec(memory_space=pl.ANY),
        scratch_shapes=[
            vmem((rows, nodes), bf16),
            vmem((full, 2 * full), bf16),
            vmem((1, full), f32),
            smem((hub_per,), i32),
            smem((2 * halo,), i32),
            smem((tiles + blocks,), i32),
            smem((tiles,), i32),
            smem((tiles,), i32),
            smem((1,), i32),
            vmem(edge_src.shape, i32),
            vmem(edge_dst.shape, i32),
            vmem((blocks + extra, rows, BLOCK), f32),
            vmem((rows, hub_per * BLOCK), bf16),
            vmem((rows, 2 * halo * BLOCK), bf16),
            vmem((rows, extra * BLOCK), bf16),
            vmem((tiles + 1, rows + 16, BLOCK), f32),
            vmem((rows, nodes), bf16),
            vmem((2 * full, quarter), bf16),
            vmem((full, quarter), bf16),
            dma((12,)),
            dma((n + 2,)),
            dma((n + 2,)),
            dma((f,)),
            dma((f,)),
            dma((f,)),
            dma((f,)),
            dma((CHUNKS, f)),
            dma((CHUNKS, f)),
            dma((CHUNKS,)),
        ],
        compiler_params=pltpu.CompilerParams(
            collective_id=0, has_side_effects=True, vmem_limit_bytes=56 * 1024 * 1024
        ),
    )(
        features,
        w_self,
        w_neigh,
        bias.reshape(1, full),
        hub_pick,
        halo_send,
        links,
        tile_src,
        tile_edges,
        tile_count,
        edge_src,
        edge_dst,
    )


def solution(mesh):
    in_specs = (
        P("feat", "graph"),
        P(),
        P(),
        P(),
        P("graph"),
        P("graph"),
        P("graph"),
        P("graph"),
        P("graph"),
        P("graph"),
        P("graph", None),
        P("graph", None),
    )
    return jax.shard_map(
        functools.partial(shards, mesh.shape["graph"], mesh.shape["feat"]),
        mesh=mesh,
        in_specs=in_specs,
        out_specs=P("feat", "graph"),
        check_vma=False,
    )
```

```python
import functools

import jax
import jax.numpy as jnp
from jax import lax
from jax.experimental import pallas as pl
from jax.experimental.pallas import tpu as pltpu
from jax.sharding import PartitionSpec as P

BLOCK = 128
GROUP = 8
CHUNKS = 2
MESH = pl.DeviceIdType.MESH


def block_at(index):
    return pl.ds(pl.multiple_of(index * BLOCK, BLOCK), BLOCK)


def layer_kernel(
    n,
    f,
    features,
    w_self,
    w_neigh,
    bias,
    hub_pick,
    halo_send,
    tile_dst,
    tile_src,
    tile_edges,
    tile_count,
    edge_src,
    edge_dst,
    out,
    feat,
    weight,
    bias_row,
    pick,
    send,
    dst,
    src,
    edges,
    count_ref,
    esrc,
    edst,
    link_rows,
    link,
    columns,
    hot,
    table,
    hub_buf,
    halo_buf,
    ext,
    running,
    means,
    joined,
    result,
    local_sem,
    send_sem,
    recv_sem,
    feat_send,
    feat_recv,
    mean_send,
    mean_recv,
    out_send,
    out_recv,
    own_sem,
):
    rows, nodes = feat.shape
    blocks = nodes // BLOCK
    total_rows = rows * f
    quarter = nodes // f
    per_quarter = quarter // BLOCK
    tiles = src.shape[0]
    hub_per = pick.shape[0]
    halo = send.shape[0] // 2
    me = lax.axis_index("graph")
    col = lax.axis_index("feat")
    high = col // 2
    low = lax.rem(col, 2)
    half = f // 2
    turns = [(a, b) for a in list(range(1, half)) + [0] for b in (0, 1) if (a, b) != (0, 0)]
    peers = [lax.rem(high + a, half) * 2 + lax.rem(low + b, 2) for a, b in turns]

    pairs = (
        (features, feat),
        (hub_pick, pick),
        (halo_send, send),
        (w_self, weight.at[:, pl.ds(0, total_rows)]),
        (w_neigh, weight.at[:, pl.ds(total_rows, total_rows)]),
        (bias, bias_row),
        (tile_dst, dst),
        (tile_src, src),
        (tile_edges, edges),
        (tile_count, count_ref),
        (edge_src, esrc),
        (edge_dst, edst),
    )
    loads = [pltpu.make_async_copy(a, b, local_sem.at[i]) for i, (a, b) in enumerate(pairs)]
    for load in loads:
        load.start()
    barrier = pltpu.get_barrier_semaphore()
    for k in range(1, n):
        pl.semaphore_signal(
            barrier, inc=1, device_id=(lax.rem(me + k, n), col), device_id_type=MESH
        )
    for peer in peers:
        pl.semaphore_signal(barrier, inc=1, device_id=(me, peer), device_id_type=MESH)
    running[0] = jnp.zeros_like(running[0])
    for load in loads[:3]:
        load.wait()
    for b in range(blocks):
        table[b] = feat[:, b * BLOCK : (b + 1) * BLOCK].astype(jnp.float32)
    for j in range(2 * halo):
        halo_buf[:, j * BLOCK : (j + 1) * BLOCK] = table[send[j]].astype(jnp.bfloat16)
    for j in range(hub_per):
        hub_buf[:, j * BLOCK : (j + 1) * BLOCK] = table[pick[j]].astype(jnp.bfloat16)
    hub_cols = hub_per * BLOCK
    halo_cols = halo * BLOCK
    own_hubs = pl.ds(pl.multiple_of(me * hub_cols, BLOCK), hub_cols)
    own_rows = pl.ds(pl.multiple_of(col * rows, rows), rows)
    own_nodes = pl.ds(pl.multiple_of(col * quarter, BLOCK), quarter)
    pl.semaphore_wait(barrier, n - 1 + f - 1)

    copies = []
    for side, peer in ((0, lax.rem(me + n - 1, n)), (1, lax.rem(me + 1, n))):
        start = n * hub_cols + (1 - side) * halo_cols
        copies.append(
            pltpu.make_async_remote_copy(
                src_ref=halo_buf.at[:, pl.ds(side * halo_cols, halo_cols)],
                dst_ref=ext.at[:, pl.ds(start, halo_cols)],
                send_sem=send_sem.at[n + side],
                recv_sem=recv_sem.at[n + side],
                device_id=(peer, col),
                device_id_type=MESH,
            )
        )
    for k in range(1, n):
        copies.append(
            pltpu.make_async_remote_copy(
                src_ref=hub_buf,
                dst_ref=ext.at[:, own_hubs],
                send_sem=send_sem.at[k],
                recv_sem=recv_sem.at[k],
                device_id=(lax.rem(me + k, n), col),
                device_id_type=MESH,
            )
        )
    for copy in copies:
        copy.start()
    feat_copies = []
    for k, peer in enumerate(peers):
        feat_copies.append(
            pltpu.make_async_remote_copy(
                src_ref=feat.at[:, pl.ds(pl.multiple_of(peer * quarter, BLOCK), quarter)],
                dst_ref=joined.at[own_rows, :],
                send_sem=feat_send.at[k],
                recv_sem=feat_recv.at[k],
                device_id=(me, peer),
                device_id_type=MESH,
            )
        )
        feat_copies[-1].start()
    joined[own_rows, :] = feat[:, own_nodes]
    ext[:, own_hubs] = hub_buf[...]
    for load in loads[3:]:
        load.wait()

    count = count_ref[0]
    square = (BLOCK, BLOCK)
    lane = lax.broadcasted_iota(jnp.int32, square, 1).astype(jnp.float32)
    sub = lax.broadcasted_iota(jnp.int32, square, 0).astype(jnp.float32)
    spans = tiles // BLOCK
    tile = lax.broadcasted_iota(jnp.int32, square, 1)
    row = lax.broadcasted_iota(jnp.int32, square, 0)
    keys = [dst[i : i + 1, :] for i in range(spans)]
    best = [jnp.zeros((1, BLOCK), jnp.int32) for _ in range(spans + 1)]
    for i in range(spans):
        spread = jnp.transpose(jnp.broadcast_to(keys[i], square))
        place = row + (i * BLOCK + 1)
        for j in range(i, spans):
            found = spread == keys[j]
            if i == j:
                found = found & (row < tile)
            best[j] = jnp.maximum(
                best[j], jnp.max(jnp.where(found, place, 0), axis=0, keepdims=True)
            )
        best[spans] = jnp.maximum(
            best[spans], jnp.max(jnp.where(spread == tile, place, 0), axis=0, keepdims=True)
        )
    link_rows[...] = jnp.zeros_like(link_rows)
    for i in range(spans + 1):
        link_rows[i : i + 1, :] = best[i]
    link_load = pltpu.make_async_copy(link_rows, link, local_sem.at[12])
    link_load.start()
    for i in range(spans):
        order = lax.broadcasted_iota(jnp.int32, (1, BLOCK), 1) + i * BLOCK
        live = jnp.where(order < count, edges[i : i + 1, :], 0).astype(jnp.float32)
        target = jnp.transpose(edst[i * BLOCK : (i + 1) * BLOCK, :].astype(jnp.float32))
        target = jnp.where(sub < live, target, -1.0)
        for k in range(BLOCK // GROUP):
            columns[i * (BLOCK // GROUP) + k] = target[:, k * GROUP : (k + 1) * GROUP]

    def build(g, carry):
        column = columns[g]
        for j in range(GROUP):
            match = jnp.broadcast_to(column[:, j : j + 1], square) == lane
            hot[g * GROUP + j] = jnp.where(match, 1.0, 0.0).astype(jnp.bfloat16)
        return carry

    lax.fori_loop(0, tiles // GROUP, build, 0)
    link_load.wait()
    for copy in copies:
        copy.wait()
    for b in range(ext.shape[1] // BLOCK):
        table[blocks + b] = ext[:, b * BLOCK : (b + 1) * BLOCK].astype(jnp.float32)
    ones = jnp.ones((16, BLOCK), jnp.bfloat16)

    def group(g, carry):
        first = pl.multiple_of(g * GROUP, GROUP)
        esrc_rows = esrc[pl.ds(first, GROUP), :]
        parts = []
        for j in range(GROUP):
            values = table[src[first + j]]
            index = jnp.broadcast_to(esrc_rows[j : j + 1, :], values.shape)
            picked = jnp.take_along_axis(values, index, axis=1, mode="promise_in_bounds")
            left = jnp.concatenate([picked.astype(jnp.bfloat16), ones], axis=0)
            parts.append(jnp.dot(left, hot[first + j], preferred_element_type=jnp.float32))
        span = g // (BLOCK // GROUP)
        spot = lax.rem(g, BLOCK // GROUP) * GROUP
        for j in range(GROUP):
            running[first + j + 1] = running[link[span, spot + j]] + parts[j]
        return carry

    lax.fori_loop(0, tiles // GROUP, group, 0)

    def quarter_means(owner):
        def finish(i, carry):
            b = owner * per_quarter + i
            total = running[link[spans, b]]
            degree = jnp.maximum(total[rows : rows + 1, :], 1.0)
            means[:, block_at(b)] = (total[:rows, :] / degree).astype(jnp.bfloat16)
            return carry

        lax.fori_loop(0, per_quarter, finish, 0, unroll=4)

    mean_rows = pl.ds(pl.multiple_of(total_rows + col * rows, rows), rows)
    mean_copies = []
    for k, peer in enumerate(peers):
        quarter_means(peer)
        mean_copies.append(
            pltpu.make_async_remote_copy(
                src_ref=means.at[:, pl.ds(pl.multiple_of(peer * quarter, BLOCK), quarter)],
                dst_ref=joined.at[mean_rows, :],
                send_sem=mean_send.at[k],
                recv_sem=mean_recv.at[k],
                device_id=(me, peer),
                device_id_type=MESH,
            )
        )
        mean_copies[-1].start()
    quarter_means(col)
    joined[mean_rows, :] = means[:, own_nodes]
    column = jnp.transpose(jnp.broadcast_to(bias_row[...], (BLOCK, total_rows)))[:, :1]
    for copy in feat_copies:
        copy.wait()
    for copy in mean_copies:
        copy.wait()
    width = quarter // CHUNKS
    out_copies = []
    own_copies = []
    for c in range(CHUNKS):
        cols = pl.ds(c * width, width)
        total = jnp.dot(weight[...], joined[:, cols], preferred_element_type=jnp.float32)
        result[:, cols] = jnp.maximum(total + column, 0.0).astype(jnp.bfloat16)
        place = pl.ds(pl.multiple_of(col * quarter + c * width, BLOCK), width)
        for k, peer in enumerate(peers):
            out_copies.append(
                pltpu.make_async_remote_copy(
                    src_ref=result.at[pl.ds(pl.multiple_of(peer * rows, rows), rows), cols],
                    dst_ref=out.at[:, place],
                    send_sem=out_send.at[c, k],
                    recv_sem=out_recv.at[c, k],
                    device_id=(me, peer),
                    device_id_type=MESH,
                )
            )
            out_copies[-1].start()
        own_copies.append(
            pltpu.make_async_copy(
                result.at[own_rows, cols], out.at[:, place], own_sem.at[c]
            )
        )
        own_copies[-1].start()
    for copy in out_copies + own_copies:
        copy.wait()


def shards(
    n,
    f,
    features,
    w_self,
    w_neigh,
    bias,
    hub_pick,
    halo_send,
    tile_dst,
    tile_src,
    tile_edges,
    tile_count,
    edge_src,
    edge_dst,
):
    rows, nodes = features.shape
    blocks = nodes // BLOCK
    tiles = tile_dst.shape[0]
    spans = tiles // BLOCK
    hub_per = hub_pick.shape[0]
    halo = halo_send.shape[0] // 2
    extra = n * hub_per + 2 * halo
    full = rows * f
    quarter = nodes // f
    bf16, f32, i32 = jnp.bfloat16, jnp.float32, jnp.int32
    vmem, smem, dma = pltpu.VMEM, pltpu.SMEM, pltpu.SemaphoreType.DMA
    return pl.pallas_call(
        functools.partial(layer_kernel, n, f),
        out_shape=jax.ShapeDtypeStruct((rows, nodes), bf16),
        in_specs=[pl.BlockSpec(memory_space=pl.ANY)] * 12,
        out_specs=pl.BlockSpec(memory_space=pl.ANY),
        scratch_shapes=[
            vmem((rows, nodes), bf16),
            vmem((full, 2 * full), bf16),
            vmem((1, full), f32),
            smem((hub_per,), i32),
            smem((2 * halo,), i32),
            vmem((spans, BLOCK), i32),
            smem((tiles,), i32),
            vmem((spans, BLOCK), i32),
            smem((1,), i32),
            vmem(edge_src.shape, i32),
            vmem(edge_dst.shape, i32),
            vmem((8, BLOCK), i32),
            smem((8, BLOCK), i32),
            vmem((tiles // GROUP, BLOCK, GROUP), f32),
            vmem((tiles, BLOCK, BLOCK), bf16),
            vmem((blocks + extra, rows, BLOCK), f32),
            vmem((rows, hub_per * BLOCK), bf16),
            vmem((rows, 2 * halo * BLOCK), bf16),
            vmem((rows, extra * BLOCK), bf16),
            vmem((tiles + 1, rows + 16, BLOCK), f32),
            vmem((rows, nodes), bf16),
            vmem((2 * full, quarter), bf16),
            vmem((full, quarter), bf16),
            dma((13,)),
            dma((n + 2,)),
            dma((n + 2,)),
            dma((f,)),
            dma((f,)),
            dma((f,)),
            dma((f,)),
            dma((CHUNKS, f)),
            dma((CHUNKS, f)),
            dma((CHUNKS,)),
        ],
        compiler_params=pltpu.CompilerParams(
            collective_id=0, has_side_effects=True, vmem_limit_bytes=56 * 1024 * 1024
        ),
    )(
        features,
        w_self,
        w_neigh,
        bias.reshape(1, full),
        hub_pick,
        halo_send,
        tile_dst.reshape(spans, BLOCK),
        tile_src,
        tile_edges.reshape(spans, BLOCK),
        tile_count,
        edge_src,
        edge_dst,
    )


def solution(mesh):
    in_specs = (
        P("feat", "graph"),
        P(),
        P(),
        P(),
        P("graph"),
        P("graph"),
        P("graph"),
        P("graph"),
        P("graph"),
        P("graph"),
        P("graph", None),
        P("graph", None),
    )
    return jax.shard_map(
        functools.partial(shards, mesh.shape["graph"], mesh.shape["feat"]),
        mesh=mesh,
        in_specs=in_specs,
        out_specs=P("feat", "graph"),
        check_vma=False,
    )
```

```python
import functools

import jax
import jax.numpy as jnp
from jax import lax
from jax.experimental import pallas as pl
from jax.experimental.pallas import tpu as pltpu
from jax.sharding import PartitionSpec as P

BLOCK = 128
GROUP = 8
STEP = 4
CHUNKS = 2
MESH = pl.DeviceIdType.MESH


def block_at(index):
    return pl.ds(pl.multiple_of(index * BLOCK, BLOCK), BLOCK)


def layer_kernel(
    n,
    f,
    features,
    w_self,
    w_neigh,
    bias,
    hub_pick,
    halo_send,
    tile_dst,
    tile_src,
    tile_edges,
    tile_count,
    edge_src,
    edge_dst,
    out,
    feat,
    weight,
    bias_row,
    pick,
    send,
    dst,
    src,
    edges,
    count_ref,
    esrc,
    edst,
    link_rows,
    link,
    columns,
    hot,
    table,
    hub_buf,
    halo_buf,
    ext,
    running,
    means,
    joined,
    result,
    local_sem,
    send_sem,
    recv_sem,
    feat_send,
    feat_recv,
    mean_send,
    mean_recv,
    out_send,
    out_recv,
    own_sem,
):
    rows, nodes = feat.shape
    blocks = nodes // BLOCK
    total_rows = rows * f
    quarter = nodes // f
    per_quarter = quarter // BLOCK
    tiles = src.shape[0]
    hub_per = pick.shape[0]
    halo = send.shape[0] // 2
    me = lax.axis_index("graph")
    col = lax.axis_index("feat")
    high = col // 2
    low = lax.rem(col, 2)
    half = f // 2
    turns = [(a, b) for a in list(range(1, half)) + [0] for b in (0, 1) if (a, b) != (0, 0)]
    peers = [lax.rem(high + a, half) * 2 + lax.rem(low + b, 2) for a, b in turns]

    pairs = (
        (features, feat),
        (hub_pick, pick),
        (halo_send, send),
        (w_self, weight.at[:, pl.ds(0, total_rows)]),
        (w_neigh, weight.at[:, pl.ds(total_rows, total_rows)]),
        (bias, bias_row),
        (tile_dst, dst),
        (tile_src, src),
        (tile_edges, edges),
        (tile_count, count_ref),
        (edge_src, esrc),
        (edge_dst, edst),
    )
    loads = [pltpu.make_async_copy(a, b, local_sem.at[i]) for i, (a, b) in enumerate(pairs)]
    for load in loads:
        load.start()
    barrier = pltpu.get_barrier_semaphore()
    for k in range(1, n):
        pl.semaphore_signal(
            barrier, inc=1, device_id=(lax.rem(me + k, n), col), device_id_type=MESH
        )
    for peer in peers:
        pl.semaphore_signal(barrier, inc=1, device_id=(me, peer), device_id_type=MESH)
    running[0] = jnp.zeros_like(running[0])
    for load in loads[:3]:
        load.wait()
    for b in range(blocks):
        table[b] = feat[:, b * BLOCK : (b + 1) * BLOCK].astype(jnp.float32)
    for j in range(2 * halo):
        halo_buf[:, j * BLOCK : (j + 1) * BLOCK] = table[send[j]].astype(jnp.bfloat16)
    for j in range(hub_per):
        hub_buf[:, j * BLOCK : (j + 1) * BLOCK] = table[pick[j]].astype(jnp.bfloat16)
    hub_cols = hub_per * BLOCK
    halo_cols = halo * BLOCK
    own_hubs = pl.ds(pl.multiple_of(me * hub_cols, BLOCK), hub_cols)
    own_rows = pl.ds(pl.multiple_of(col * rows, rows), rows)
    own_nodes = pl.ds(pl.multiple_of(col * quarter, BLOCK), quarter)
    pl.semaphore_wait(barrier, n - 1 + f - 1)

    copies = []
    for side, peer in ((0, lax.rem(me + n - 1, n)), (1, lax.rem(me + 1, n))):
        start = n * hub_cols + (1 - side) * halo_cols
        copies.append(
            pltpu.make_async_remote_copy(
                src_ref=halo_buf.at[:, pl.ds(side * halo_cols, halo_cols)],
                dst_ref=ext.at[:, pl.ds(start, halo_cols)],
                send_sem=send_sem.at[n + side],
                recv_sem=recv_sem.at[n + side],
                device_id=(peer, col),
                device_id_type=MESH,
            )
        )
    for k in range(1, n):
        copies.append(
            pltpu.make_async_remote_copy(
                src_ref=hub_buf,
                dst_ref=ext.at[:, own_hubs],
                send_sem=send_sem.at[k],
                recv_sem=recv_sem.at[k],
                device_id=(lax.rem(me + k, n), col),
                device_id_type=MESH,
            )
        )
    for copy in copies:
        copy.start()
    feat_copies = []
    for k, peer in enumerate(peers):
        feat_copies.append(
            pltpu.make_async_remote_copy(
                src_ref=feat.at[:, pl.ds(pl.multiple_of(peer * quarter, BLOCK), quarter)],
                dst_ref=joined.at[own_rows, :],
                send_sem=feat_send.at[k],
                recv_sem=feat_recv.at[k],
                device_id=(me, peer),
                device_id_type=MESH,
            )
        )
        feat_copies[-1].start()
    joined[own_rows, :] = feat[:, own_nodes]
    ext[:, own_hubs] = hub_buf[...]
    for load in loads[3:]:
        load.wait()

    count = count_ref[0]
    square = (BLOCK, BLOCK)
    lane = lax.broadcasted_iota(jnp.int32, square, 1).astype(jnp.float32)
    sub = lax.broadcasted_iota(jnp.int32, square, 0).astype(jnp.float32)
    spans = tiles // BLOCK
    tile = lax.broadcasted_iota(jnp.int32, square, 1)
    row = lax.broadcasted_iota(jnp.int32, square, 0)
    keys = [dst[i : i + 1, :] for i in range(spans)]
    best = [jnp.zeros((1, BLOCK), jnp.int32) for _ in range(spans + 1)]
    for i in range(spans):
        spread = jnp.transpose(jnp.broadcast_to(keys[i], square))
        place = row + (i * BLOCK + 1)
        for j in range(i, spans):
            found = spread == keys[j]
            if i == j:
                found = found & (row < tile)
            best[j] = jnp.maximum(
                best[j], jnp.max(jnp.where(found, place, 0), axis=0, keepdims=True)
            )
        best[spans] = jnp.maximum(
            best[spans], jnp.max(jnp.where(spread == tile, place, 0), axis=0, keepdims=True)
        )
    link_rows[...] = jnp.zeros_like(link_rows)
    for i in range(spans + 1):
        link_rows[i : i + 1, :] = best[i]
    link_load = pltpu.make_async_copy(link_rows, link, local_sem.at[12])
    link_load.start()
    for i in range(spans):
        order = lax.broadcasted_iota(jnp.int32, (1, BLOCK), 1) + i * BLOCK
        live = jnp.where(order < count, edges[i : i + 1, :], 0).astype(jnp.float32)
        target = jnp.transpose(edst[i * BLOCK : (i + 1) * BLOCK, :].astype(jnp.float32))
        target = jnp.where(sub < live, target, -1.0)
        for k in range(BLOCK // GROUP):
            columns[i * (BLOCK // GROUP) + k] = target[:, k * GROUP : (k + 1) * GROUP]

    def build(g, carry):
        for i in range(2):
            column = columns[g * 2 + i]
            for j in range(GROUP):
                match = jnp.broadcast_to(column[:, j : j + 1], square) == lane
                hot[(g * 2 + i) * GROUP + j] = jnp.where(match, 1.0, 0.0).astype(jnp.bfloat16)
        return carry

    lax.fori_loop(0, tiles // (2 * GROUP), build, 0)
    link_load.wait()
    for copy in copies:
        copy.wait()
    for b in range(ext.shape[1] // BLOCK):
        table[blocks + b] = ext[:, b * BLOCK : (b + 1) * BLOCK].astype(jnp.float32)
    ones = jnp.ones((16, BLOCK), jnp.bfloat16)

    def group(g, carry):
        first = pl.multiple_of(g * (STEP * GROUP), STEP * GROUP)
        parts = []
        for i in range(STEP):
            esrc_rows = esrc[pl.ds(first + i * GROUP, GROUP), :]
            for j in range(GROUP):
                t = first + i * GROUP + j
                values = table[src[t]]
                index = jnp.broadcast_to(esrc_rows[j : j + 1, :], values.shape)
                picked = jnp.take_along_axis(values, index, axis=1, mode="promise_in_bounds")
                left = jnp.concatenate([picked.astype(jnp.bfloat16), ones], axis=0)
                parts.append(jnp.dot(left, hot[t], preferred_element_type=jnp.float32))
        span = first // BLOCK
        spot = lax.rem(first, BLOCK)
        for j in range(STEP * GROUP):
            running[first + j + 1] = running[link[span, spot + j]] + parts[j]
        return carry

    lax.fori_loop(0, tiles // (STEP * GROUP), group, 0)

    width = quarter // CHUNKS
    per_chunk = width // BLOCK

    def chunk_means(owner, c):
        for i in range(per_chunk):
            b = owner * per_quarter + c * per_chunk + i
            total = running[link[spans, b]]
            degree = jnp.maximum(total[rows : rows + 1, :], 1.0)
            means[:, block_at(b)] = (total[:rows, :] / degree).astype(jnp.bfloat16)

    mean_rows = pl.ds(pl.multiple_of(total_rows + col * rows, rows), rows)
    mean_copies = []
    for c in range(CHUNKS):
        cols = pl.ds(c * width, width)
        for k, peer in enumerate(peers):
            chunk_means(peer, c)
            spot = pl.ds(pl.multiple_of(peer * quarter + c * width, BLOCK), width)
            mean_copies.append(
                pltpu.make_async_remote_copy(
                    src_ref=means.at[:, spot],
                    dst_ref=joined.at[mean_rows, cols],
                    send_sem=mean_send.at[c, k],
                    recv_sem=mean_recv.at[c, k],
                    device_id=(me, peer),
                    device_id_type=MESH,
                )
            )
            mean_copies[-1].start()
    for c in range(CHUNKS):
        chunk_means(col, c)
    joined[mean_rows, :] = means[:, own_nodes]
    column = jnp.transpose(jnp.broadcast_to(bias_row[...], (BLOCK, total_rows)))[:, :1]
    for copy in feat_copies:
        copy.wait()
    out_copies = []
    own_copies = []
    for c in range(CHUNKS):
        cols = pl.ds(c * width, width)
        for copy in mean_copies[c * len(peers) : (c + 1) * len(peers)]:
            copy.wait()
        total = jnp.dot(weight[...], joined[:, cols], preferred_element_type=jnp.float32)
        result[:, cols] = (total + column).astype(jnp.bfloat16)
        place = pl.ds(pl.multiple_of(col * quarter + c * width, BLOCK), width)
        for k, peer in enumerate(peers):
            out_copies.append(
                pltpu.make_async_remote_copy(
                    src_ref=result.at[pl.ds(pl.multiple_of(peer * rows, rows), rows), cols],
                    dst_ref=out.at[:, place],
                    send_sem=out_send.at[c, k],
                    recv_sem=out_recv.at[c, k],
                    device_id=(me, peer),
                    device_id_type=MESH,
                )
            )
            out_copies[-1].start()
        own_copies.append(
            pltpu.make_async_copy(
                result.at[own_rows, cols], out.at[:, place], own_sem.at[c]
            )
        )
        own_copies[-1].start()
    for copy in out_copies + own_copies:
        copy.wait()


def shards(
    n,
    f,
    features,
    w_self,
    w_neigh,
    bias,
    hub_pick,
    halo_send,
    tile_dst,
    tile_src,
    tile_edges,
    tile_count,
    edge_src,
    edge_dst,
):
    rows, nodes = features.shape
    blocks = nodes // BLOCK
    tiles = tile_dst.shape[0]
    spans = tiles // BLOCK
    hub_per = hub_pick.shape[0]
    halo = halo_send.shape[0] // 2
    extra = n * hub_per + 2 * halo
    full = rows * f
    quarter = nodes // f
    bf16, f32, i32 = jnp.bfloat16, jnp.float32, jnp.int32
    vmem, smem, dma = pltpu.VMEM, pltpu.SMEM, pltpu.SemaphoreType.DMA
    total = pl.pallas_call(
        functools.partial(layer_kernel, n, f),
        out_shape=jax.ShapeDtypeStruct((rows, nodes), bf16),
        in_specs=[pl.BlockSpec(memory_space=pl.ANY)] * 12,
        out_specs=pl.BlockSpec(memory_space=pl.ANY),
        scratch_shapes=[
            vmem((rows, nodes), bf16),
            vmem((full, 2 * full), bf16),
            vmem((1, full), f32),
            smem((hub_per,), i32),
            smem((2 * halo,), i32),
            vmem((spans, BLOCK), i32),
            smem((tiles,), i32),
            vmem((spans, BLOCK), i32),
            smem((1,), i32),
            vmem(edge_src.shape, i32),
            vmem(edge_dst.shape, i32),
            vmem((8, BLOCK), i32),
            smem((8, BLOCK), i32),
            vmem((tiles // GROUP, BLOCK, GROUP), f32),
            vmem((tiles, BLOCK, BLOCK), bf16),
            vmem((blocks + extra, rows, BLOCK), f32),
            vmem((rows, hub_per * BLOCK), bf16),
            vmem((rows, 2 * halo * BLOCK), bf16),
            vmem((rows, extra * BLOCK), bf16),
            vmem((tiles + 1, rows + 16, BLOCK), f32),
            vmem((rows, nodes), bf16),
            vmem((2 * full, quarter), bf16),
            vmem((full, quarter), bf16),
            dma((13,)),
            dma((n + 2,)),
            dma((n + 2,)),
            dma((f,)),
            dma((f,)),
            dma((CHUNKS, f)),
            dma((CHUNKS, f)),
            dma((CHUNKS, f)),
            dma((CHUNKS, f)),
            dma((CHUNKS,)),
        ],
        compiler_params=pltpu.CompilerParams(
            collective_id=0, has_side_effects=True, vmem_limit_bytes=56 * 1024 * 1024
        ),
    )(
        features,
        w_self,
        w_neigh,
        bias.reshape(1, full),
        hub_pick,
        halo_send,
        tile_dst.reshape(spans, BLOCK),
        tile_src,
        tile_edges.reshape(spans, BLOCK),
        tile_count,
        edge_src,
        edge_dst,
    )
    return jax.nn.relu(total)


def solution(mesh):
    in_specs = (
        P("feat", "graph"),
        P(),
        P(),
        P(),
        P("graph"),
        P("graph"),
        P("graph"),
        P("graph"),
        P("graph"),
        P("graph"),
        P("graph", None),
        P("graph", None),
    )
    return jax.shard_map(
        functools.partial(shards, mesh.shape["graph"], mesh.shape["feat"]),
        mesh=mesh,
        in_specs=in_specs,
        out_specs=P("feat", "graph"),
        check_vma=False,
    )
```

```python
import functools

import jax
import jax.numpy as jnp
from jax import lax
from jax.experimental import pallas as pl
from jax.experimental.pallas import tpu as pltpu
from jax.sharding import PartitionSpec as P

BLOCK = 128
GROUP = 8
STEP = 8
CHUNKS = 4
PIECES = 4
MESH = pl.DeviceIdType.MESH


def block_at(index):
    return pl.ds(pl.multiple_of(index * BLOCK, BLOCK), BLOCK)


def layer_kernel(
    n,
    f,
    features,
    w_self,
    w_neigh,
    bias,
    hub_pick,
    halo_send,
    tile_dst,
    tile_src,
    tile_edges,
    tile_count,
    edge_src,
    edge_dst,
    out,
    feat,
    weight,
    bias_row,
    pick,
    send,
    dst,
    src,
    edges,
    count_ref,
    esrc,
    edst,
    link_rows,
    link,
    columns,
    hot,
    table,
    hub_buf,
    halo_buf,
    ext,
    running,
    means,
    joined,
    result,
    local_sem,
    send_sem,
    recv_sem,
    feat_send,
    feat_recv,
    mean_send,
    mean_recv,
    out_send,
    out_recv,
    own_sem,
):
    rows, nodes = feat.shape
    blocks = nodes // BLOCK
    total_rows = rows * f
    quarter = nodes // f
    per_quarter = quarter // BLOCK
    tiles = src.shape[0]
    hub_per = pick.shape[0]
    halo = send.shape[0] // 2
    me = lax.axis_index("graph")
    col = lax.axis_index("feat")
    high = col // 2
    low = lax.rem(col, 2)
    half = f // 2
    turns = [(a, b) for a in list(range(1, half)) + [0] for b in (0, 1) if (a, b) != (0, 0)]
    peers = [lax.rem(high + a, half) * 2 + lax.rem(low + b, 2) for a, b in turns]

    barrier = pltpu.get_barrier_semaphore()
    for k in range(1, n):
        pl.semaphore_signal(
            barrier, inc=1, device_id=(lax.rem(me + k, n), col), device_id_type=MESH
        )
    for peer in peers:
        pl.semaphore_signal(barrier, inc=1, device_id=(me, peer), device_id_type=MESH)
    pairs = (
        (features, feat),
        (hub_pick, pick),
        (halo_send, send),
        (w_self, weight.at[:, pl.ds(0, total_rows)]),
        (w_neigh, weight.at[:, pl.ds(total_rows, total_rows)]),
        (bias, bias_row),
        (tile_dst, dst),
        (tile_src, src),
        (tile_edges, edges),
        (tile_count, count_ref),
        (edge_src, esrc),
        (edge_dst, edst),
    )
    loads = [pltpu.make_async_copy(a, b, local_sem.at[i]) for i, (a, b) in enumerate(pairs)]
    for load in loads:
        load.start()
    running[0] = jnp.zeros_like(running[0])
    for load in loads[:3]:
        load.wait()
    for b in range(blocks):
        table[b] = feat[:, b * BLOCK : (b + 1) * BLOCK].astype(jnp.float32)
    for j in range(2 * halo):
        halo_buf[:, j * BLOCK : (j + 1) * BLOCK] = table[send[j]].astype(jnp.bfloat16)
    for j in range(hub_per):
        hub_buf[:, j * BLOCK : (j + 1) * BLOCK] = table[pick[j]].astype(jnp.bfloat16)
    hub_cols = hub_per * BLOCK
    halo_cols = halo * BLOCK
    own_hubs = pl.ds(pl.multiple_of(me * hub_cols, BLOCK), hub_cols)
    own_rows = pl.ds(pl.multiple_of(col * rows, rows), rows)
    own_nodes = pl.ds(pl.multiple_of(col * quarter, BLOCK), quarter)
    pl.semaphore_wait(barrier, n - 1 + f - 1)

    copies = []
    for side, peer in ((0, lax.rem(me + n - 1, n)), (1, lax.rem(me + 1, n))):
        start = n * hub_cols + (1 - side) * halo_cols
        copies.append(
            pltpu.make_async_remote_copy(
                src_ref=halo_buf.at[:, pl.ds(side * halo_cols, halo_cols)],
                dst_ref=ext.at[:, pl.ds(start, halo_cols)],
                send_sem=send_sem.at[n + side],
                recv_sem=recv_sem.at[n + side],
                device_id=(peer, col),
                device_id_type=MESH,
            )
        )
    for k in range(1, n):
        copies.append(
            pltpu.make_async_remote_copy(
                src_ref=hub_buf,
                dst_ref=ext.at[:, own_hubs],
                send_sem=send_sem.at[k],
                recv_sem=recv_sem.at[k],
                device_id=(lax.rem(me + k, n), col),
                device_id_type=MESH,
            )
        )
    for copy in copies:
        copy.start()
    feat_copies = []
    for k, peer in enumerate(peers):
        feat_copies.append(
            pltpu.make_async_remote_copy(
                src_ref=feat.at[:, pl.ds(pl.multiple_of(peer * quarter, BLOCK), quarter)],
                dst_ref=joined.at[own_rows, :],
                send_sem=feat_send.at[k],
                recv_sem=feat_recv.at[k],
                device_id=(me, peer),
                device_id_type=MESH,
            )
        )
        feat_copies[-1].start()
    joined[own_rows, :] = feat[:, own_nodes]
    ext[:, own_hubs] = hub_buf[...]
    for load in loads[3:]:
        load.wait()

    count = count_ref[0]
    square = (BLOCK, BLOCK)
    lane = lax.broadcasted_iota(jnp.int32, square, 1).astype(jnp.float32)
    sub = lax.broadcasted_iota(jnp.int32, square, 0).astype(jnp.float32)
    spans = tiles // BLOCK
    tile = lax.broadcasted_iota(jnp.int32, square, 1)
    row = lax.broadcasted_iota(jnp.int32, square, 0)
    keys = [dst[i : i + 1, :] for i in range(spans)]
    best = [jnp.zeros((1, BLOCK), jnp.int32) for _ in range(spans + 1)]
    for i in range(spans):
        spread = jnp.transpose(jnp.broadcast_to(keys[i], square))
        place = row + (i * BLOCK + 1)
        for j in range(i, spans):
            found = spread == keys[j]
            if i == j:
                found = found & (row < tile)
            best[j] = jnp.maximum(
                best[j], jnp.max(jnp.where(found, place, 0), axis=0, keepdims=True)
            )
        best[spans] = jnp.maximum(
            best[spans], jnp.max(jnp.where(spread == tile, place, 0), axis=0, keepdims=True)
        )
    link_rows[...] = jnp.zeros_like(link_rows)
    for i in range(spans + 1):
        link_rows[i : i + 1, :] = best[i]
    link_load = pltpu.make_async_copy(link_rows, link, local_sem.at[12])
    link_load.start()
    for i in range(spans):
        order = lax.broadcasted_iota(jnp.int32, (1, BLOCK), 1) + i * BLOCK
        live = jnp.where(order < count, edges[i : i + 1, :], 0).astype(jnp.float32)
        target = jnp.transpose(edst[i * BLOCK : (i + 1) * BLOCK, :].astype(jnp.float32))
        target = jnp.where(sub < live, target, -1.0)
        for k in range(BLOCK // GROUP):
            columns[i * (BLOCK // GROUP) + k] = target[:, k * GROUP : (k + 1) * GROUP]

    def build(g, carry):
        for i in range(2):
            column = columns[g * 2 + i]
            for j in range(GROUP):
                match = jnp.broadcast_to(column[:, j : j + 1], square) == lane
                hot[(g * 2 + i) * GROUP + j] = jnp.where(match, 1.0, 0.0).astype(jnp.bfloat16)
        return carry

    lax.fori_loop(0, tiles // (2 * GROUP), build, 0)
    link_load.wait()
    for copy in copies:
        copy.wait()
    for b in range(ext.shape[1] // BLOCK):
        table[blocks + b] = ext[:, b * BLOCK : (b + 1) * BLOCK].astype(jnp.float32)
    ones = jnp.ones((16, BLOCK), jnp.bfloat16)

    def group(g, carry):
        first = pl.multiple_of(g * (STEP * GROUP), STEP * GROUP)
        parts = []
        for i in range(STEP):
            esrc_rows = esrc[pl.ds(first + i * GROUP, GROUP), :]
            for j in range(GROUP):
                t = first + i * GROUP + j
                values = table[src[t]]
                index = jnp.broadcast_to(esrc_rows[j : j + 1, :], values.shape)
                picked = jnp.take_along_axis(values, index, axis=1, mode="promise_in_bounds")
                left = jnp.concatenate([picked.astype(jnp.bfloat16), ones], axis=0)
                parts.append(jnp.dot(left, hot[t], preferred_element_type=jnp.float32))
        span = first // BLOCK
        spot = lax.rem(first, BLOCK)
        for j in range(STEP * GROUP):
            running[first + j + 1] = running[link[span, spot + j]] + parts[j]
        return carry

    lax.fori_loop(0, tiles // (STEP * GROUP), group, 0)

    width = quarter // CHUNKS
    per_chunk = width // BLOCK

    def chunk_means(owner, c):
        for i in range(per_chunk):
            b = owner * per_quarter + c * per_chunk + i
            total = running[link[spans, b]]
            degree = jnp.maximum(total[rows : rows + 1, :], 1.0)
            means[:, block_at(b)] = (total[:rows, :] / degree).astype(jnp.bfloat16)

    mean_rows = pl.ds(pl.multiple_of(total_rows + col * rows, rows), rows)
    mean_copies = []
    for c in range(CHUNKS):
        cols = pl.ds(c * width, width)
        for k, peer in enumerate(peers):
            chunk_means(peer, c)
            spot = pl.ds(pl.multiple_of(peer * quarter + c * width, BLOCK), width)
            mean_copies.append(
                pltpu.make_async_remote_copy(
                    src_ref=means.at[:, spot],
                    dst_ref=joined.at[mean_rows, cols],
                    send_sem=mean_send.at[c, k],
                    recv_sem=mean_recv.at[c, k],
                    device_id=(me, peer),
                    device_id_type=MESH,
                )
            )
            mean_copies[-1].start()
    for c in range(CHUNKS):
        chunk_means(col, c)
    joined[mean_rows, :] = means[:, own_nodes]
    column = jnp.transpose(jnp.broadcast_to(bias_row[...], (BLOCK, total_rows)))[:, :1]
    for copy in feat_copies:
        copy.wait()
    out_copies = []
    own_copies = []
    for c in range(CHUNKS):
        cols = pl.ds(c * width, width)
        for copy in mean_copies[c * len(peers) : (c + 1) * len(peers)]:
            copy.wait()
        total = jnp.dot(weight[...], joined[:, cols], preferred_element_type=jnp.float32)
        result[:, cols] = jnp.maximum(total + column, 0.0).astype(jnp.bfloat16)
        place = pl.ds(pl.multiple_of(col * quarter + c * width, BLOCK), width)
        for k, peer in enumerate(peers):
            out_copies.append(
                pltpu.make_async_remote_copy(
                    src_ref=result.at[pl.ds(pl.multiple_of(peer * rows, rows), rows), cols],
                    dst_ref=out.at[:, place],
                    send_sem=out_send.at[c, k],
                    recv_sem=out_recv.at[c, k],
                    device_id=(me, peer),
                    device_id_type=MESH,
                )
            )
            out_copies[-1].start()
        own_copies.append(
            pltpu.make_async_copy(
                result.at[own_rows, cols], out.at[:, place], own_sem.at[c]
            )
        )
        own_copies[-1].start()
    for copy in out_copies + own_copies:
        copy.wait()


def hand_on_kernel(held, out, sem):
    width = held.shape[1] // PIECES
    copies = [
        pltpu.make_async_copy(
            held.at[:, pl.ds(i * width, width)], out.at[:, pl.ds(i * width, width)], sem.at[i]
        )
        for i in range(PIECES)
    ]
    for copy in copies:
        copy.start()
    for copy in copies:
        copy.wait()


def hand_on(held):
    return pl.pallas_call(
        hand_on_kernel,
        out_shape=jax.ShapeDtypeStruct(held.shape, held.dtype),
        in_specs=[pl.BlockSpec(memory_space=pl.ANY)],
        out_specs=pl.BlockSpec(memory_space=pl.ANY),
        scratch_shapes=[pltpu.SemaphoreType.DMA((PIECES,))],
        compiler_params=pltpu.CompilerParams(vmem_limit_bytes=56 * 1024 * 1024),
    )(held)


def shards(
    n,
    f,
    features,
    w_self,
    w_neigh,
    bias,
    hub_pick,
    halo_send,
    tile_dst,
    tile_src,
    tile_edges,
    tile_count,
    edge_src,
    edge_dst,
):
    rows, nodes = features.shape
    blocks = nodes // BLOCK
    tiles = tile_dst.shape[0]
    spans = tiles // BLOCK
    hub_per = hub_pick.shape[0]
    halo = halo_send.shape[0] // 2
    extra = n * hub_per + 2 * halo
    full = rows * f
    quarter = nodes // f
    bf16, f32, i32 = jnp.bfloat16, jnp.float32, jnp.int32
    vmem, smem, dma = pltpu.VMEM, pltpu.SMEM, pltpu.SemaphoreType.DMA
    total = pl.pallas_call(
        functools.partial(layer_kernel, n, f),
        out_shape=jax.ShapeDtypeStruct((rows, nodes), bf16),
        in_specs=[pl.BlockSpec(memory_space=pl.ANY)] * 12,
        out_specs=pl.BlockSpec(memory_space=pl.ANY),
        scratch_shapes=[
            vmem((rows, nodes), bf16),
            vmem((full, 2 * full), bf16),
            vmem((1, full), f32),
            smem((hub_per,), i32),
            smem((2 * halo,), i32),
            vmem((spans, BLOCK), i32),
            smem((tiles,), i32),
            vmem((spans, BLOCK), i32),
            smem((1,), i32),
            vmem(edge_src.shape, i32),
            vmem(edge_dst.shape, i32),
            vmem((8, BLOCK), i32),
            smem((8, BLOCK), i32),
            vmem((tiles // GROUP, BLOCK, GROUP), f32),
            vmem((tiles, BLOCK, BLOCK), bf16),
            vmem((blocks + extra, rows, BLOCK), f32),
            vmem((rows, hub_per * BLOCK), bf16),
            vmem((rows, 2 * halo * BLOCK), bf16),
            vmem((rows, extra * BLOCK), bf16),
            vmem((tiles + 1, rows + 16, BLOCK), f32),
            vmem((rows, nodes), bf16),
            vmem((2 * full, quarter), bf16),
            vmem((full, quarter), bf16),
            dma((13,)),
            dma((n + 2,)),
            dma((n + 2,)),
            dma((f,)),
            dma((f,)),
            dma((CHUNKS, f)),
            dma((CHUNKS, f)),
            dma((CHUNKS, f)),
            dma((CHUNKS, f)),
            dma((CHUNKS,)),
        ],
        compiler_params=pltpu.CompilerParams(
            collective_id=0, has_side_effects=True, vmem_limit_bytes=56 * 1024 * 1024
        ),
    )(
        features,
        w_self,
        w_neigh,
        bias.reshape(1, full),
        hub_pick,
        halo_send,
        tile_dst.reshape(spans, BLOCK),
        tile_src,
        tile_edges.reshape(spans, BLOCK),
        tile_count,
        edge_src,
        edge_dst,
    )
    return hand_on(total)


def solution(mesh):
    in_specs = (
        P("feat", "graph"),
        P(),
        P(),
        P(),
        P("graph"),
        P("graph"),
        P("graph"),
        P("graph"),
        P("graph"),
        P("graph"),
        P("graph", None),
        P("graph", None),
    )
    return jax.shard_map(
        functools.partial(shards, mesh.shape["graph"], mesh.shape["feat"]),
        mesh=mesh,
        in_specs=in_specs,
        out_specs=P("feat", "graph"),
        check_vma=False,
    )
```

```python
import functools

import jax
import jax.numpy as jnp
from jax import lax
from jax.experimental import pallas as pl
from jax.experimental.pallas import tpu as pltpu
from jax.sharding import PartitionSpec as P

BLOCK = 128
GROUP = 8
STEP = 8
CHUNKS = 4
MESH = pl.DeviceIdType.MESH


def block_at(index):
    return pl.ds(pl.multiple_of(index * BLOCK, BLOCK), BLOCK)


def layer_kernel(
    n,
    f,
    features,
    w_self,
    w_neigh,
    bias,
    hub_pick,
    halo_send,
    tile_dst,
    tile_src,
    tile_edges,
    tile_count,
    edge_src,
    edge_dst,
    out,
    feat,
    weight,
    bias_row,
    pick,
    send,
    dst,
    src,
    edges,
    count_ref,
    esrc,
    edst,
    link_rows,
    link,
    columns,
    hot,
    table,
    hub_buf,
    halo_buf,
    ext,
    running,
    means,
    joined,
    result,
    local_sem,
    send_sem,
    recv_sem,
    feat_send,
    feat_recv,
    mean_send,
    mean_recv,
    out_send,
    out_recv,
    own_sem,
):
    rows, nodes = feat.shape
    blocks = nodes // BLOCK
    total_rows = rows * f
    quarter = nodes // f
    per_quarter = quarter // BLOCK
    tiles = src.shape[0]
    hub_per = pick.shape[0]
    halo = send.shape[0] // 2
    me = lax.axis_index("graph")
    col = lax.axis_index("feat")
    high = col // 2
    low = lax.rem(col, 2)
    half = f // 2
    turns = [(a, b) for a in list(range(1, half)) + [0] for b in (0, 1) if (a, b) != (0, 0)]
    peers = [lax.rem(high + a, half) * 2 + lax.rem(low + b, 2) for a, b in turns]

    barrier = pltpu.get_barrier_semaphore()
    for k in range(1, n):
        pl.semaphore_signal(
            barrier, inc=1, device_id=(lax.rem(me + k, n), col), device_id_type=MESH
        )
    for peer in peers:
        pl.semaphore_signal(barrier, inc=1, device_id=(me, peer), device_id_type=MESH)
    pairs = (
        (features, feat),
        (hub_pick, pick),
        (halo_send, send),
        (w_self, weight.at[:, pl.ds(0, total_rows)]),
        (w_neigh, weight.at[:, pl.ds(total_rows, total_rows)]),
        (bias, bias_row),
        (tile_dst, dst),
        (tile_src, src),
        (tile_edges, edges),
        (tile_count, count_ref),
        (edge_src, esrc),
        (edge_dst, edst),
    )
    loads = [pltpu.make_async_copy(a, b, local_sem.at[i]) for i, (a, b) in enumerate(pairs)]
    for load in loads:
        load.start()
    running[0] = jnp.zeros_like(running[0])
    for load in loads[:3]:
        load.wait()
    for b in range(blocks):
        table[b] = feat[:, b * BLOCK : (b + 1) * BLOCK].astype(jnp.float32)
    for j in range(2 * halo):
        halo_buf[:, j * BLOCK : (j + 1) * BLOCK] = table[send[j]].astype(jnp.bfloat16)
    for j in range(hub_per):
        hub_buf[:, j * BLOCK : (j + 1) * BLOCK] = table[pick[j]].astype(jnp.bfloat16)
    hub_cols = hub_per * BLOCK
    halo_cols = halo * BLOCK
    own_hubs = pl.ds(pl.multiple_of(me * hub_cols, BLOCK), hub_cols)
    own_rows = pl.ds(pl.multiple_of(col * rows, rows), rows)
    own_nodes = pl.ds(pl.multiple_of(col * quarter, BLOCK), quarter)
    pl.semaphore_wait(barrier, n - 1 + f - 1)

    copies = []
    for side, peer in ((0, lax.rem(me + n - 1, n)), (1, lax.rem(me + 1, n))):
        start = n * hub_cols + (1 - side) * halo_cols
        copies.append(
            pltpu.make_async_remote_copy(
                src_ref=halo_buf.at[:, pl.ds(side * halo_cols, halo_cols)],
                dst_ref=ext.at[:, pl.ds(start, halo_cols)],
                send_sem=send_sem.at[n + side],
                recv_sem=recv_sem.at[n + side],
                device_id=(peer, col),
                device_id_type=MESH,
            )
        )
    for k in range(1, n):
        copies.append(
            pltpu.make_async_remote_copy(
                src_ref=hub_buf,
                dst_ref=ext.at[:, own_hubs],
                send_sem=send_sem.at[k],
                recv_sem=recv_sem.at[k],
                device_id=(lax.rem(me + k, n), col),
                device_id_type=MESH,
            )
        )
    for copy in copies:
        copy.start()
    feat_copies = []
    for k, peer in enumerate(peers):
        feat_copies.append(
            pltpu.make_async_remote_copy(
                src_ref=feat.at[:, pl.ds(pl.multiple_of(peer * quarter, BLOCK), quarter)],
                dst_ref=joined.at[own_rows, :],
                send_sem=feat_send.at[k],
                recv_sem=feat_recv.at[k],
                device_id=(me, peer),
                device_id_type=MESH,
            )
        )
        feat_copies[-1].start()
    joined[own_rows, :] = feat[:, own_nodes]
    ext[:, own_hubs] = hub_buf[...]
    for load in loads[3:]:
        load.wait()

    count = count_ref[0]
    square = (BLOCK, BLOCK)
    lane = lax.broadcasted_iota(jnp.int32, square, 1).astype(jnp.float32)
    sub = lax.broadcasted_iota(jnp.int32, square, 0).astype(jnp.float32)
    spans = tiles // BLOCK
    tile = lax.broadcasted_iota(jnp.int32, square, 1)
    row = lax.broadcasted_iota(jnp.int32, square, 0)
    keys = [dst[i : i + 1, :] for i in range(spans)]
    best = [jnp.zeros((1, BLOCK), jnp.int32) for _ in range(spans + 1)]
    for i in range(spans):
        spread = jnp.transpose(jnp.broadcast_to(keys[i], square))
        place = row + (i * BLOCK + 1)
        for j in range(i, spans):
            found = spread == keys[j]
            if i == j:
                found = found & (row < tile)
            best[j] = jnp.maximum(
                best[j], jnp.max(jnp.where(found, place, 0), axis=0, keepdims=True)
            )
        best[spans] = jnp.maximum(
            best[spans], jnp.max(jnp.where(spread == tile, place, 0), axis=0, keepdims=True)
        )
    link_rows[...] = jnp.zeros_like(link_rows)
    for i in range(spans + 1):
        link_rows[i : i + 1, :] = best[i]
    link_load = pltpu.make_async_copy(link_rows, link, local_sem.at[12])
    link_load.start()
    for i in range(spans):
        order = lax.broadcasted_iota(jnp.int32, (1, BLOCK), 1) + i * BLOCK
        live = jnp.where(order < count, edges[i : i + 1, :], 0).astype(jnp.float32)
        target = jnp.transpose(edst[i * BLOCK : (i + 1) * BLOCK, :].astype(jnp.float32))
        target = jnp.where(sub < live, target, -1.0)
        for k in range(BLOCK // GROUP):
            columns[i * (BLOCK // GROUP) + k] = target[:, k * GROUP : (k + 1) * GROUP]

    def build(g, carry):
        for i in range(2):
            column = columns[g * 2 + i]
            for j in range(GROUP):
                match = jnp.broadcast_to(column[:, j : j + 1], square) == lane
                hot[(g * 2 + i) * GROUP + j] = jnp.where(match, 1.0, 0.0).astype(jnp.bfloat16)
        return carry

    lax.fori_loop(0, tiles // (2 * GROUP), build, 0)
    link_load.wait()
    for copy in copies:
        copy.wait()
    for b in range(ext.shape[1] // BLOCK):
        table[blocks + b] = ext[:, b * BLOCK : (b + 1) * BLOCK].astype(jnp.float32)
    ones = jnp.ones((16, BLOCK), jnp.bfloat16)

    def group(g, carry):
        first = pl.multiple_of(g * (STEP * GROUP), STEP * GROUP)
        parts = []
        for i in range(STEP):
            esrc_rows = esrc[pl.ds(first + i * GROUP, GROUP), :]
            for j in range(GROUP):
                t = first + i * GROUP + j
                values = table[src[t]]
                index = jnp.broadcast_to(esrc_rows[j : j + 1, :], values.shape)
                picked = jnp.take_along_axis(values, index, axis=1, mode="promise_in_bounds")
                left = jnp.concatenate([picked.astype(jnp.bfloat16), ones], axis=0)
                parts.append(jnp.dot(left, hot[t], preferred_element_type=jnp.float32))
        span = first // BLOCK
        spot = lax.rem(first, BLOCK)
        for j in range(STEP * GROUP):
            running[first + j + 1] = running[link[span, spot + j]] + parts[j]
        return carry

    lax.fori_loop(0, tiles // (STEP * GROUP), group, 0)

    width = quarter // CHUNKS
    per_chunk = width // BLOCK

    def chunk_means(owner, c):
        for i in range(per_chunk):
            b = owner * per_quarter + c * per_chunk + i
            total = running[link[spans, b]]
            degree = jnp.maximum(total[rows : rows + 1, :], 1.0)
            means[:, block_at(b)] = (total[:rows, :] / degree).astype(jnp.bfloat16)

    mean_rows = pl.ds(pl.multiple_of(total_rows + col * rows, rows), rows)
    mean_copies = []
    for c in range(CHUNKS):
        cols = pl.ds(c * width, width)
        for k, peer in enumerate(peers):
            chunk_means(peer, c)
            spot = pl.ds(pl.multiple_of(peer * quarter + c * width, BLOCK), width)
            mean_copies.append(
                pltpu.make_async_remote_copy(
                    src_ref=means.at[:, spot],
                    dst_ref=joined.at[mean_rows, cols],
                    send_sem=mean_send.at[c, k],
                    recv_sem=mean_recv.at[c, k],
                    device_id=(me, peer),
                    device_id_type=MESH,
                )
            )
            mean_copies[-1].start()
    for c in range(CHUNKS):
        chunk_means(col, c)
    joined[mean_rows, :] = means[:, own_nodes]
    column = jnp.transpose(jnp.broadcast_to(bias_row[...], (BLOCK, total_rows)))[:, :1]
    for copy in feat_copies:
        copy.wait()
    out_copies = []
    own_copies = []
    for c in range(CHUNKS):
        cols = pl.ds(c * width, width)
        for copy in mean_copies[c * len(peers) : (c + 1) * len(peers)]:
            copy.wait()
        total = jnp.dot(weight[...], joined[:, cols], preferred_element_type=jnp.float32)
        result[:, cols] = jnp.maximum(total + column, 0.0).astype(jnp.bfloat16)
        place = pl.ds(pl.multiple_of(col * quarter + c * width, BLOCK), width)
        for k, peer in enumerate(peers):
            out_copies.append(
                pltpu.make_async_remote_copy(
                    src_ref=result.at[pl.ds(pl.multiple_of(peer * rows, rows), rows), cols],
                    dst_ref=out.at[:, place],
                    send_sem=out_send.at[c, k],
                    recv_sem=out_recv.at[c, k],
                    device_id=(me, peer),
                    device_id_type=MESH,
                )
            )
            out_copies[-1].start()
        own_copies.append(
            pltpu.make_async_copy(
                result.at[own_rows, cols], out.at[:, place], own_sem.at[c]
            )
        )
        own_copies[-1].start()
    for copy in out_copies + own_copies:
        copy.wait()


def shards(
    n,
    f,
    features,
    w_self,
    w_neigh,
    bias,
    hub_pick,
    halo_send,
    tile_dst,
    tile_src,
    tile_edges,
    tile_count,
    edge_src,
    edge_dst,
):
    rows, nodes = features.shape
    blocks = nodes // BLOCK
    tiles = tile_dst.shape[0]
    spans = tiles // BLOCK
    hub_per = hub_pick.shape[0]
    halo = halo_send.shape[0] // 2
    extra = n * hub_per + 2 * halo
    full = rows * f
    quarter = nodes // f
    bf16, f32, i32 = jnp.bfloat16, jnp.float32, jnp.int32
    vmem, smem, dma = pltpu.VMEM, pltpu.SMEM, pltpu.SemaphoreType.DMA
    return pl.pallas_call(
        functools.partial(layer_kernel, n, f),
        out_shape=vmem((rows, nodes), bf16),
        in_specs=[pl.BlockSpec(memory_space=pl.ANY)] * 12,
        out_specs=pl.BlockSpec(memory_space=pltpu.VMEM),
        scratch_shapes=[
            vmem((rows, nodes), bf16),
            vmem((full, 2 * full), bf16),
            vmem((1, full), f32),
            smem((hub_per,), i32),
            smem((2 * halo,), i32),
            vmem((spans, BLOCK), i32),
            smem((tiles,), i32),
            vmem((spans, BLOCK), i32),
            smem((1,), i32),
            vmem(edge_src.shape, i32),
            vmem(edge_dst.shape, i32),
            vmem((8, BLOCK), i32),
            smem((8, BLOCK), i32),
            vmem((tiles // GROUP, BLOCK, GROUP), f32),
            vmem((tiles, BLOCK, BLOCK), bf16),
            vmem((blocks + extra, rows, BLOCK), f32),
            vmem((rows, hub_per * BLOCK), bf16),
            vmem((rows, 2 * halo * BLOCK), bf16),
            vmem((rows, extra * BLOCK), bf16),
            vmem((tiles + 1, rows + 16, BLOCK), f32),
            vmem((rows, nodes), bf16),
            vmem((2 * full, quarter), bf16),
            vmem((full, quarter), bf16),
            dma((13,)),
            dma((n + 2,)),
            dma((n + 2,)),
            dma((f,)),
            dma((f,)),
            dma((CHUNKS, f)),
            dma((CHUNKS, f)),
            dma((CHUNKS, f)),
            dma((CHUNKS, f)),
            dma((CHUNKS,)),
        ],
        compiler_params=pltpu.CompilerParams(
            collective_id=0, has_side_effects=True, vmem_limit_bytes=56 * 1024 * 1024
        ),
    )(
        features,
        w_self,
        w_neigh,
        bias.reshape(1, full),
        hub_pick,
        halo_send,
        tile_dst.reshape(spans, BLOCK),
        tile_src,
        tile_edges.reshape(spans, BLOCK),
        tile_count,
        edge_src,
        edge_dst,
    )


def solution(mesh):
    in_specs = (
        P("feat", "graph"),
        P(),
        P(),
        P(),
        P("graph"),
        P("graph"),
        P("graph"),
        P("graph"),
        P("graph"),
        P("graph"),
        P("graph", None),
        P("graph", None),
    )
    return jax.shard_map(
        functools.partial(shards, mesh.shape["graph"], mesh.shape["feat"]),
        mesh=mesh,
        in_specs=in_specs,
        out_specs=P("feat", "graph"),
        check_vma=False,
    )
```

```python
import functools

import jax
import jax.numpy as jnp
from jax import lax
from jax.experimental import pallas as pl
from jax.experimental.pallas import tpu as pltpu
from jax.sharding import PartitionSpec as P

BLOCK = 128
GROUP = 8
STEP = 8
CHUNKS = 4
MESH = pl.DeviceIdType.MESH


def block_at(index):
    return pl.ds(pl.multiple_of(index * BLOCK, BLOCK), BLOCK)


def layer_kernel(
    n,
    f,
    features,
    w_self,
    w_neigh,
    bias,
    hub_pick,
    halo_send,
    tile_dst,
    tile_src,
    tile_edges,
    tile_count,
    edge_src,
    edge_dst,
    out,
    feat,
    weight,
    bias_row,
    pick,
    send,
    dst,
    src,
    edges,
    count_ref,
    esrc,
    edst,
    link_rows,
    link,
    columns,
    hot,
    table,
    hub_buf,
    halo_buf,
    ext,
    running,
    means,
    joined,
    result,
    local_sem,
    send_sem,
    recv_sem,
    feat_send,
    feat_recv,
    mean_send,
    mean_recv,
    out_send,
    out_recv,
    own_sem,
):
    rows, nodes = feat.shape
    blocks = nodes // BLOCK
    total_rows = rows * f
    quarter = nodes // f
    per_quarter = quarter // BLOCK
    tiles = src.shape[0]
    hub_per = pick.shape[0]
    halo = send.shape[0] // 2
    me = lax.axis_index("graph")
    col = lax.axis_index("feat")
    high = col // 2
    low = lax.rem(col, 2)
    half = f // 2
    turns = [(a, b) for a in list(range(1, half)) + [0] for b in (0, 1) if (a, b) != (0, 0)]
    peers = [lax.rem(high + a, half) * 2 + lax.rem(low + b, 2) for a, b in turns]

    barrier = pltpu.get_barrier_semaphore()
    for k in range(1, n):
        pl.semaphore_signal(
            barrier, inc=1, device_id=(lax.rem(me + k, n), col), device_id_type=MESH
        )
    for peer in peers:
        pl.semaphore_signal(barrier, inc=1, device_id=(me, peer), device_id_type=MESH)
    pairs = (
        (features, feat),
        (hub_pick, pick),
        (halo_send, send),
        (w_self, weight.at[:, pl.ds(0, total_rows)]),
        (w_neigh, weight.at[:, pl.ds(total_rows, total_rows)]),
        (bias, bias_row),
        (tile_dst, dst),
        (tile_src, src),
        (tile_edges, edges),
        (tile_count, count_ref),
        (edge_src, esrc),
        (edge_dst, edst),
    )
    loads = [pltpu.make_async_copy(a, b, local_sem.at[i]) for i, (a, b) in enumerate(pairs)]
    for load in loads:
        load.start()
    running[0] = jnp.zeros_like(running[0])
    for load in loads[:3]:
        load.wait()
    for b in range(blocks):
        table[b] = feat[:, b * BLOCK : (b + 1) * BLOCK].astype(jnp.float32)
    for j in range(2 * halo):
        halo_buf[:, j * BLOCK : (j + 1) * BLOCK] = table[send[j]].astype(jnp.bfloat16)
    for j in range(hub_per):
        hub_buf[:, j * BLOCK : (j + 1) * BLOCK] = table[pick[j]].astype(jnp.bfloat16)
    hub_cols = hub_per * BLOCK
    halo_cols = halo * BLOCK
    own_hubs = pl.ds(pl.multiple_of(me * hub_cols, BLOCK), hub_cols)
    own_rows = pl.ds(pl.multiple_of(col * rows, rows), rows)
    own_nodes = pl.ds(pl.multiple_of(col * quarter, BLOCK), quarter)
    pl.semaphore_wait(barrier, n - 1 + f - 1)

    copies = []
    for side, peer in ((0, lax.rem(me + n - 1, n)), (1, lax.rem(me + 1, n))):
        start = n * hub_cols + (1 - side) * halo_cols
        copies.append(
            pltpu.make_async_remote_copy(
                src_ref=halo_buf.at[:, pl.ds(side * halo_cols, halo_cols)],
                dst_ref=ext.at[:, pl.ds(start, halo_cols)],
                send_sem=send_sem.at[n + side],
                recv_sem=recv_sem.at[n + side],
                device_id=(peer, col),
                device_id_type=MESH,
            )
        )
    for k in range(1, n):
        copies.append(
            pltpu.make_async_remote_copy(
                src_ref=hub_buf,
                dst_ref=ext.at[:, own_hubs],
                send_sem=send_sem.at[k],
                recv_sem=recv_sem.at[k],
                device_id=(lax.rem(me + k, n), col),
                device_id_type=MESH,
            )
        )
    for copy in copies:
        copy.start()
    feat_copies = []
    for k, peer in enumerate(peers):
        feat_copies.append(
            pltpu.make_async_remote_copy(
                src_ref=feat.at[:, pl.ds(pl.multiple_of(peer * quarter, BLOCK), quarter)],
                dst_ref=joined.at[own_rows, :],
                send_sem=feat_send.at[k],
                recv_sem=feat_recv.at[k],
                device_id=(me, peer),
                device_id_type=MESH,
            )
        )
        feat_copies[-1].start()
    joined[own_rows, :] = feat[:, own_nodes]
    ext[:, own_hubs] = hub_buf[...]
    for load in loads[3:]:
        load.wait()

    count = count_ref[0]
    square = (BLOCK, BLOCK)
    lane = lax.broadcasted_iota(jnp.int32, square, 1).astype(jnp.float32)
    sub = lax.broadcasted_iota(jnp.int32, square, 0).astype(jnp.float32)
    spans = tiles // BLOCK
    tile = lax.broadcasted_iota(jnp.int32, square, 1)
    row = lax.broadcasted_iota(jnp.int32, square, 0)
    keys = [dst[i : i + 1, :] for i in range(spans)]
    best = [jnp.zeros((1, BLOCK), jnp.int32) for _ in range(spans + 1)]
    for i in range(spans):
        spread = jnp.transpose(jnp.broadcast_to(keys[i], square))
        place = row + (i * BLOCK + 1)
        for j in range(i, spans):
            found = spread == keys[j]
            if i == j:
                found = found & (row < tile)
            best[j] = jnp.maximum(
                best[j], jnp.max(jnp.where(found, place, 0), axis=0, keepdims=True)
            )
        best[spans] = jnp.maximum(
            best[spans], jnp.max(jnp.where(spread == tile, place, 0), axis=0, keepdims=True)
        )
    link_rows[...] = jnp.zeros_like(link_rows)
    for i in range(spans + 1):
        link_rows[i : i + 1, :] = best[i]
    link_load = pltpu.make_async_copy(link_rows, link, local_sem.at[12])
    link_load.start()
    for i in range(spans):
        order = lax.broadcasted_iota(jnp.int32, (1, BLOCK), 1) + i * BLOCK
        live = jnp.where(order < count, edges[i : i + 1, :], 0).astype(jnp.float32)
        target = jnp.transpose(edst[i * BLOCK : (i + 1) * BLOCK, :].astype(jnp.float32))
        target = jnp.where(sub < live, target, -1.0)
        for k in range(BLOCK // GROUP):
            columns[i * (BLOCK // GROUP) + k] = target[:, k * GROUP : (k + 1) * GROUP]

    def build(g, carry):
        for i in range(2):
            column = columns[g * 2 + i]
            for j in range(GROUP):
                match = jnp.broadcast_to(column[:, j : j + 1], square) == lane
                hot[(g * 2 + i) * GROUP + j] = jnp.where(match, 1.0, 0.0).astype(jnp.bfloat16)
        return carry

    lax.fori_loop(0, tiles // (2 * GROUP), build, 0)
    link_load.wait()
    for copy in copies:
        copy.wait()
    for b in range(ext.shape[1] // BLOCK):
        table[blocks + b] = ext[:, b * BLOCK : (b + 1) * BLOCK].astype(jnp.float32)
    ones = jnp.ones((16, BLOCK), jnp.bfloat16)

    def group(g, carry):
        first = pl.multiple_of(g * (STEP * GROUP), STEP * GROUP)
        parts = []
        for i in range(STEP):
            esrc_rows = esrc[pl.ds(first + i * GROUP, GROUP), :]
            for j in range(GROUP):
                t = first + i * GROUP + j
                values = table[src[t]]
                index = jnp.broadcast_to(esrc_rows[j : j + 1, :], values.shape)
                picked = jnp.take_along_axis(values, index, axis=1, mode="promise_in_bounds")
                left = jnp.concatenate([picked.astype(jnp.bfloat16), ones], axis=0)
                part = jnp.dot(left, hot[t], preferred_element_type=jnp.float32)
                parts.append(part[: rows + 8])
        span = first // BLOCK
        spot = lax.rem(first, BLOCK)
        for j in range(STEP * GROUP):
            running[first + j + 1] = running[link[span, spot + j]] + parts[j]
        return carry

    lax.fori_loop(0, tiles // (STEP * GROUP), group, 0)

    width = quarter // CHUNKS
    per_chunk = width // BLOCK

    def chunk_means(owner, c):
        for i in range(per_chunk):
            b = owner * per_quarter + c * per_chunk + i
            total = running[link[spans, b]]
            degree = jnp.maximum(total[rows : rows + 1, :], 1.0)
            means[:, block_at(b)] = (total[:rows, :] / degree).astype(jnp.bfloat16)

    mean_rows = pl.ds(pl.multiple_of(total_rows + col * rows, rows), rows)
    mean_copies = []
    for c in range(CHUNKS):
        cols = pl.ds(c * width, width)
        for k, peer in enumerate(peers):
            chunk_means(peer, c)
            spot = pl.ds(pl.multiple_of(peer * quarter + c * width, BLOCK), width)
            mean_copies.append(
                pltpu.make_async_remote_copy(
                    src_ref=means.at[:, spot],
                    dst_ref=joined.at[mean_rows, cols],
                    send_sem=mean_send.at[c, k],
                    recv_sem=mean_recv.at[c, k],
                    device_id=(me, peer),
                    device_id_type=MESH,
                )
            )
            mean_copies[-1].start()
    for c in range(CHUNKS):
        chunk_means(col, c)
    joined[mean_rows, :] = means[:, own_nodes]
    column = jnp.transpose(jnp.broadcast_to(bias_row[...], (BLOCK, total_rows)))[:, :1]
    for copy in feat_copies:
        copy.wait()
    out_copies = []
    own_copies = []
    for c in range(CHUNKS):
        cols = pl.ds(c * width, width)
        for copy in mean_copies[c * len(peers) : (c + 1) * len(peers)]:
            copy.wait()
        total = jnp.dot(weight[...], joined[:, cols], preferred_element_type=jnp.float32)
        result[:, cols] = jnp.maximum(total + column, 0.0).astype(jnp.bfloat16)
        place = pl.ds(pl.multiple_of(col * quarter + c * width, BLOCK), width)
        for k, peer in enumerate(peers):
            out_copies.append(
                pltpu.make_async_remote_copy(
                    src_ref=result.at[pl.ds(pl.multiple_of(peer * rows, rows), rows), cols],
                    dst_ref=out.at[:, place],
                    send_sem=out_send.at[c, k],
                    recv_sem=out_recv.at[c, k],
                    device_id=(me, peer),
                    device_id_type=MESH,
                )
            )
            out_copies[-1].start()
        own_copies.append(
            pltpu.make_async_copy(
                result.at[own_rows, cols], out.at[:, place], own_sem.at[c]
            )
        )
        own_copies[-1].start()
    for copy in out_copies + own_copies:
        copy.wait()


def shards(
    n,
    f,
    features,
    w_self,
    w_neigh,
    bias,
    hub_pick,
    halo_send,
    tile_dst,
    tile_src,
    tile_edges,
    tile_count,
    edge_src,
    edge_dst,
):
    rows, nodes = features.shape
    blocks = nodes // BLOCK
    tiles = tile_dst.shape[0]
    spans = tiles // BLOCK
    hub_per = hub_pick.shape[0]
    halo = halo_send.shape[0] // 2
    extra = n * hub_per + 2 * halo
    full = rows * f
    quarter = nodes // f
    bf16, f32, i32 = jnp.bfloat16, jnp.float32, jnp.int32
    vmem, smem, dma = pltpu.VMEM, pltpu.SMEM, pltpu.SemaphoreType.DMA
    return pl.pallas_call(
        functools.partial(layer_kernel, n, f),
        out_shape=vmem((rows, nodes), bf16),
        in_specs=[pl.BlockSpec(memory_space=pl.ANY)] * 12,
        out_specs=pl.BlockSpec(memory_space=pltpu.VMEM),
        scratch_shapes=[
            vmem((rows, nodes), bf16),
            vmem((full, 2 * full), bf16),
            vmem((1, full), f32),
            smem((hub_per,), i32),
            smem((2 * halo,), i32),
            vmem((spans, BLOCK), i32),
            smem((tiles,), i32),
            vmem((spans, BLOCK), i32),
            smem((1,), i32),
            vmem(edge_src.shape, i32),
            vmem(edge_dst.shape, i32),
            vmem((8, BLOCK), i32),
            smem((8, BLOCK), i32),
            vmem((tiles // GROUP, BLOCK, GROUP), f32),
            vmem((tiles, BLOCK, BLOCK), bf16),
            vmem((blocks + extra, rows, BLOCK), f32),
            vmem((rows, hub_per * BLOCK), bf16),
            vmem((rows, 2 * halo * BLOCK), bf16),
            vmem((rows, extra * BLOCK), bf16),
            vmem((tiles + 1, rows + 8, BLOCK), f32),
            vmem((rows, nodes), bf16),
            vmem((2 * full, quarter), bf16),
            vmem((full, quarter), bf16),
            dma((13,)),
            dma((n + 2,)),
            dma((n + 2,)),
            dma((f,)),
            dma((f,)),
            dma((CHUNKS, f)),
            dma((CHUNKS, f)),
            dma((CHUNKS, f)),
            dma((CHUNKS, f)),
            dma((CHUNKS,)),
        ],
        compiler_params=pltpu.CompilerParams(
            collective_id=0, has_side_effects=True, vmem_limit_bytes=56 * 1024 * 1024
        ),
    )(
        features,
        w_self,
        w_neigh,
        bias.reshape(1, full),
        hub_pick,
        halo_send,
        tile_dst.reshape(spans, BLOCK),
        tile_src,
        tile_edges.reshape(spans, BLOCK),
        tile_count,
        edge_src,
        edge_dst,
    )


def solution(mesh):
    in_specs = (
        P("feat", "graph"),
        P(),
        P(),
        P(),
        P("graph"),
        P("graph"),
        P("graph"),
        P("graph"),
        P("graph"),
        P("graph"),
        P("graph", None),
        P("graph", None),
    )
    return jax.shard_map(
        functools.partial(shards, mesh.shape["graph"], mesh.shape["feat"]),
        mesh=mesh,
        in_specs=in_specs,
        out_specs=P("feat", "graph"),
        check_vma=False,
    )
```

```python
import functools

import jax
import jax.numpy as jnp
from jax import lax
from jax.experimental import pallas as pl
from jax.experimental.pallas import tpu as pltpu
from jax.sharding import PartitionSpec as P

BLOCK = 128
GROUP = 8
STEP = 8
CHUNKS = 4
MESH = pl.DeviceIdType.MESH


def block_at(index):
    return pl.ds(pl.multiple_of(index * BLOCK, BLOCK), BLOCK)


def lane_gather(values, index):
    numbers = lax.GatherDimensionNumbers(
        offset_dims=(),
        collapsed_slice_dims=(1,),
        start_index_map=(1,),
        operand_batching_dims=(0,),
        start_indices_batching_dims=(0,),
    )
    return lax.gather(
        values,
        index[..., None],
        numbers,
        slice_sizes=(1, 1),
        mode=lax.GatherScatterMode.PROMISE_IN_BOUNDS,
    )


def layer_kernel(
    n,
    f,
    features,
    w_self,
    w_neigh,
    bias,
    hub_pick,
    halo_send,
    tile_dst,
    tile_src,
    tile_edges,
    tile_count,
    edge_src,
    edge_dst,
    out,
    feat,
    weight,
    bias_row,
    pick,
    send,
    dst,
    src,
    edges,
    count_ref,
    esrc,
    edst,
    link_rows,
    link,
    columns,
    hot,
    table,
    hub_buf,
    halo_buf,
    ext,
    running,
    means,
    joined,
    result,
    local_sem,
    send_sem,
    recv_sem,
    feat_send,
    feat_recv,
    mean_send,
    mean_recv,
    out_send,
    out_recv,
    own_sem,
):
    rows, nodes = feat.shape
    blocks = nodes // BLOCK
    total_rows = rows * f
    quarter = nodes // f
    per_quarter = quarter // BLOCK
    tiles = src.shape[0]
    hub_per = pick.shape[0]
    halo = send.shape[0] // 2
    me = lax.axis_index("graph")
    col = lax.axis_index("feat")
    high = col // 2
    low = lax.rem(col, 2)
    half = f // 2
    turns = [(a, b) for a in list(range(1, half)) + [0] for b in (0, 1) if (a, b) != (0, 0)]
    peers = [lax.rem(high + a, half) * 2 + lax.rem(low + b, 2) for a, b in turns]

    barrier = pltpu.get_barrier_semaphore()
    for k in range(1, n):
        pl.semaphore_signal(
            barrier, inc=1, device_id=(lax.rem(me + k, n), col), device_id_type=MESH
        )
    for peer in peers:
        pl.semaphore_signal(barrier, inc=1, device_id=(me, peer), device_id_type=MESH)
    pairs = (
        (features, feat),
        (hub_pick, pick),
        (halo_send, send),
        (w_self, weight.at[:, pl.ds(0, total_rows)]),
        (w_neigh, weight.at[:, pl.ds(total_rows, total_rows)]),
        (bias, bias_row),
        (tile_dst, dst),
        (tile_src, src),
        (tile_edges, edges),
        (tile_count, count_ref),
        (edge_src, esrc),
        (edge_dst, edst),
    )
    loads = [pltpu.make_async_copy(a, b, local_sem.at[i]) for i, (a, b) in enumerate(pairs)]
    for load in loads:
        load.start()
    running[0] = jnp.zeros_like(running[0])
    for load in loads[:3]:
        load.wait()
    for b in range(blocks):
        table[b] = feat[:, b * BLOCK : (b + 1) * BLOCK]
    for j in range(2 * halo):
        halo_buf[:, j * BLOCK : (j + 1) * BLOCK] = table[send[j]]
    for j in range(hub_per):
        hub_buf[:, j * BLOCK : (j + 1) * BLOCK] = table[pick[j]]
    hub_cols = hub_per * BLOCK
    halo_cols = halo * BLOCK
    own_hubs = pl.ds(pl.multiple_of(me * hub_cols, BLOCK), hub_cols)
    own_rows = pl.ds(pl.multiple_of(col * rows, rows), rows)
    own_nodes = pl.ds(pl.multiple_of(col * quarter, BLOCK), quarter)
    pl.semaphore_wait(barrier, n - 1 + f - 1)

    copies = []
    for side, peer in ((0, lax.rem(me + n - 1, n)), (1, lax.rem(me + 1, n))):
        start = n * hub_cols + (1 - side) * halo_cols
        copies.append(
            pltpu.make_async_remote_copy(
                src_ref=halo_buf.at[:, pl.ds(side * halo_cols, halo_cols)],
                dst_ref=ext.at[:, pl.ds(start, halo_cols)],
                send_sem=send_sem.at[n + side],
                recv_sem=recv_sem.at[n + side],
                device_id=(peer, col),
                device_id_type=MESH,
            )
        )
    for k in range(1, n):
        copies.append(
            pltpu.make_async_remote_copy(
                src_ref=hub_buf,
                dst_ref=ext.at[:, own_hubs],
                send_sem=send_sem.at[k],
                recv_sem=recv_sem.at[k],
                device_id=(lax.rem(me + k, n), col),
                device_id_type=MESH,
            )
        )
    for copy in copies:
        copy.start()
    feat_copies = []
    for k, peer in enumerate(peers):
        feat_copies.append(
            pltpu.make_async_remote_copy(
                src_ref=feat.at[:, pl.ds(pl.multiple_of(peer * quarter, BLOCK), quarter)],
                dst_ref=joined.at[own_rows, :],
                send_sem=feat_send.at[k],
                recv_sem=feat_recv.at[k],
                device_id=(me, peer),
                device_id_type=MESH,
            )
        )
        feat_copies[-1].start()
    joined[own_rows, :] = feat[:, own_nodes]
    ext[:, own_hubs] = hub_buf[...]
    for load in loads[3:]:
        load.wait()

    count = count_ref[0]
    square = (BLOCK, BLOCK)
    lane = lax.broadcasted_iota(jnp.int32, square, 1).astype(jnp.float32)
    sub = lax.broadcasted_iota(jnp.int32, square, 0).astype(jnp.float32)
    spans = tiles // BLOCK
    tile = lax.broadcasted_iota(jnp.int32, square, 1)
    row = lax.broadcasted_iota(jnp.int32, square, 0)
    keys = [dst[i : i + 1, :] for i in range(spans)]
    best = [jnp.zeros((1, BLOCK), jnp.int32) for _ in range(spans + 1)]
    for i in range(spans):
        spread = jnp.transpose(jnp.broadcast_to(keys[i], square))
        place = row + (i * BLOCK + 1)
        for j in range(i, spans):
            found = spread == keys[j]
            if i == j:
                found = found & (row < tile)
            best[j] = jnp.maximum(
                best[j], jnp.max(jnp.where(found, place, 0), axis=0, keepdims=True)
            )
        best[spans] = jnp.maximum(
            best[spans], jnp.max(jnp.where(spread == tile, place, 0), axis=0, keepdims=True)
        )
    link_rows[...] = jnp.zeros_like(link_rows)
    for i in range(spans + 1):
        link_rows[i : i + 1, :] = best[i]
    link_load = pltpu.make_async_copy(link_rows, link, local_sem.at[12])
    link_load.start()
    for i in range(spans):
        order = lax.broadcasted_iota(jnp.int32, (1, BLOCK), 1) + i * BLOCK
        live = jnp.where(order < count, edges[i : i + 1, :], 0).astype(jnp.float32)
        target = jnp.transpose(edst[i * BLOCK : (i + 1) * BLOCK, :].astype(jnp.float32))
        target = jnp.where(sub < live, target, -1.0)
        for k in range(BLOCK // GROUP):
            columns[i * (BLOCK // GROUP) + k] = target[:, k * GROUP : (k + 1) * GROUP]

    def build(g, carry):
        for i in range(2):
            column = columns[g * 2 + i]
            for j in range(GROUP):
                match = jnp.broadcast_to(column[:, j : j + 1], square) == lane
                hot[(g * 2 + i) * GROUP + j] = jnp.where(match, 1.0, 0.0).astype(jnp.bfloat16)
        return carry

    lax.fori_loop(0, tiles // (2 * GROUP), build, 0)
    link_load.wait()
    for copy in copies:
        copy.wait()
    for b in range(ext.shape[1] // BLOCK):
        table[blocks + b] = ext[:, b * BLOCK : (b + 1) * BLOCK]
    ones = jnp.ones((16, BLOCK), jnp.bfloat16)

    def group(g, carry):
        first = pl.multiple_of(g * (STEP * GROUP), STEP * GROUP)
        parts = []
        for i in range(STEP):
            esrc_rows = esrc[pl.ds(first + i * GROUP, GROUP), :]
            for j in range(GROUP):
                t = first + i * GROUP + j
                values = table[src[t]]
                index = jnp.broadcast_to(esrc_rows[j : j + 1, :], values.shape).astype(jnp.int16)
                picked = lane_gather(values, index)
                left = jnp.concatenate([picked, ones], axis=0)
                part = jnp.dot(left, hot[t], preferred_element_type=jnp.float32)
                parts.append(part[: rows + 8])
        span = first // BLOCK
        spot = lax.rem(first, BLOCK)
        for j in range(STEP * GROUP):
            running[first + j + 1] = running[link[span, spot + j]] + parts[j]
        return carry

    lax.fori_loop(0, tiles // (STEP * GROUP), group, 0)

    width = quarter // CHUNKS
    per_chunk = width // BLOCK

    def chunk_means(owner, c):
        for i in range(per_chunk):
            b = owner * per_quarter + c * per_chunk + i
            total = running[link[spans, b]]
            degree = jnp.maximum(total[rows : rows + 1, :], 1.0)
            means[:, block_at(b)] = (total[:rows, :] / degree).astype(jnp.bfloat16)

    mean_rows = pl.ds(pl.multiple_of(total_rows + col * rows, rows), rows)
    mean_copies = []
    for c in range(CHUNKS):
        cols = pl.ds(c * width, width)
        for k, peer in enumerate(peers):
            chunk_means(peer, c)
            spot = pl.ds(pl.multiple_of(peer * quarter + c * width, BLOCK), width)
            mean_copies.append(
                pltpu.make_async_remote_copy(
                    src_ref=means.at[:, spot],
                    dst_ref=joined.at[mean_rows, cols],
                    send_sem=mean_send.at[c, k],
                    recv_sem=mean_recv.at[c, k],
                    device_id=(me, peer),
                    device_id_type=MESH,
                )
            )
            mean_copies[-1].start()
    for c in range(CHUNKS):
        chunk_means(col, c)
    joined[mean_rows, :] = means[:, own_nodes]
    column = jnp.transpose(jnp.broadcast_to(bias_row[...], (BLOCK, total_rows)))[:, :1]
    for copy in feat_copies:
        copy.wait()
    out_copies = []
    own_copies = []
    for c in range(CHUNKS):
        cols = pl.ds(c * width, width)
        for copy in mean_copies[c * len(peers) : (c + 1) * len(peers)]:
            copy.wait()
        total = jnp.dot(weight[...], joined[:, cols], preferred_element_type=jnp.float32)
        result[:, cols] = jnp.maximum(total + column, 0.0).astype(jnp.bfloat16)
        place = pl.ds(pl.multiple_of(col * quarter + c * width, BLOCK), width)
        for k, peer in enumerate(peers):
            out_copies.append(
                pltpu.make_async_remote_copy(
                    src_ref=result.at[pl.ds(pl.multiple_of(peer * rows, rows), rows), cols],
                    dst_ref=out.at[:, place],
                    send_sem=out_send.at[c, k],
                    recv_sem=out_recv.at[c, k],
                    device_id=(me, peer),
                    device_id_type=MESH,
                )
            )
            out_copies[-1].start()
        own_copies.append(
            pltpu.make_async_copy(
                result.at[own_rows, cols], out.at[:, place], own_sem.at[c]
            )
        )
        own_copies[-1].start()
    for copy in out_copies + own_copies:
        copy.wait()


def shards(
    n,
    f,
    features,
    w_self,
    w_neigh,
    bias,
    hub_pick,
    halo_send,
    tile_dst,
    tile_src,
    tile_edges,
    tile_count,
    edge_src,
    edge_dst,
):
    rows, nodes = features.shape
    blocks = nodes // BLOCK
    tiles = tile_dst.shape[0]
    spans = tiles // BLOCK
    hub_per = hub_pick.shape[0]
    halo = halo_send.shape[0] // 2
    extra = n * hub_per + 2 * halo
    full = rows * f
    quarter = nodes // f
    bf16, f32, i32 = jnp.bfloat16, jnp.float32, jnp.int32
    vmem, smem, dma = pltpu.VMEM, pltpu.SMEM, pltpu.SemaphoreType.DMA
    return pl.pallas_call(
        functools.partial(layer_kernel, n, f),
        out_shape=vmem((rows, nodes), bf16),
        in_specs=[pl.BlockSpec(memory_space=pl.ANY)] * 12,
        out_specs=pl.BlockSpec(memory_space=pltpu.VMEM),
        scratch_shapes=[
            vmem((rows, nodes), bf16),
            vmem((full, 2 * full), bf16),
            vmem((1, full), f32),
            smem((hub_per,), i32),
            smem((2 * halo,), i32),
            vmem((spans, BLOCK), i32),
            smem((tiles,), i32),
            vmem((spans, BLOCK), i32),
            smem((1,), i32),
            vmem(edge_src.shape, i32),
            vmem(edge_dst.shape, i32),
            vmem((8, BLOCK), i32),
            smem((8, BLOCK), i32),
            vmem((tiles // GROUP, BLOCK, GROUP), f32),
            vmem((tiles, BLOCK, BLOCK), bf16),
            vmem((blocks + extra, rows, BLOCK), bf16),
            vmem((rows, hub_per * BLOCK), bf16),
            vmem((rows, 2 * halo * BLOCK), bf16),
            vmem((rows, extra * BLOCK), bf16),
            vmem((tiles + 1, rows + 8, BLOCK), f32),
            vmem((rows, nodes), bf16),
            vmem((2 * full, quarter), bf16),
            vmem((full, quarter), bf16),
            dma((13,)),
            dma((n + 2,)),
            dma((n + 2,)),
            dma((f,)),
            dma((f,)),
            dma((CHUNKS, f)),
            dma((CHUNKS, f)),
            dma((CHUNKS, f)),
            dma((CHUNKS, f)),
            dma((CHUNKS,)),
        ],
        compiler_params=pltpu.CompilerParams(
            collective_id=0, has_side_effects=True, vmem_limit_bytes=56 * 1024 * 1024
        ),
    )(
        features,
        w_self,
        w_neigh,
        bias.reshape(1, full),
        hub_pick,
        halo_send,
        tile_dst.reshape(spans, BLOCK),
        tile_src,
        tile_edges.reshape(spans, BLOCK),
        tile_count,
        edge_src,
        edge_dst,
    )


def solution(mesh):
    in_specs = (
        P("feat", "graph"),
        P(),
        P(),
        P(),
        P("graph"),
        P("graph"),
        P("graph"),
        P("graph"),
        P("graph"),
        P("graph"),
        P("graph", None),
        P("graph", None),
    )
    return jax.shard_map(
        functools.partial(shards, mesh.shape["graph"], mesh.shape["feat"]),
        mesh=mesh,
        in_specs=in_specs,
        out_specs=P("feat", "graph"),
        check_vma=False,
    )
```

```python
import functools

import jax
import jax.numpy as jnp
from jax import lax
from jax.experimental import pallas as pl
from jax.experimental.pallas import tpu as pltpu
from jax.sharding import PartitionSpec as P

BLOCK = 128
GROUP = 8
STEP = 8
CHUNKS = 4
MESH = pl.DeviceIdType.MESH


def block_at(index):
    return pl.ds(pl.multiple_of(index * BLOCK, BLOCK), BLOCK)


def lane_gather(values, index):
    numbers = lax.GatherDimensionNumbers(
        offset_dims=(),
        collapsed_slice_dims=(1,),
        start_index_map=(1,),
        operand_batching_dims=(0,),
        start_indices_batching_dims=(0,),
    )
    return lax.gather(
        values,
        index[..., None],
        numbers,
        slice_sizes=(1, 1),
        mode=lax.GatherScatterMode.PROMISE_IN_BOUNDS,
    )


def layer_kernel(
    n,
    f,
    features,
    w_self,
    w_neigh,
    bias,
    hub_pick,
    halo_send,
    tile_dst,
    tile_src,
    tile_edges,
    tile_count,
    edge_src,
    edge_dst,
    out,
    feat,
    weight,
    bias_row,
    pick,
    send,
    dst,
    src,
    edges,
    count_ref,
    esrc,
    edst,
    link_rows,
    link,
    columns,
    hot,
    table,
    hub_buf,
    halo_buf,
    ext,
    running,
    means,
    joined,
    result,
    local_sem,
    send_sem,
    recv_sem,
    feat_send,
    feat_recv,
    mean_send,
    mean_recv,
    out_send,
    out_recv,
    own_sem,
):
    rows, nodes = feat.shape
    blocks = nodes // BLOCK
    total_rows = rows * f
    quarter = nodes // f
    per_quarter = quarter // BLOCK
    tiles = src.shape[0]
    hub_per = pick.shape[0]
    halo = send.shape[0] // 2
    me = lax.axis_index("graph")
    col = lax.axis_index("feat")
    high = col // 2
    low = lax.rem(col, 2)
    half = f // 2
    turns = [(a, b) for a in list(range(1, half)) + [0] for b in (0, 1) if (a, b) != (0, 0)]
    peers = [lax.rem(high + a, half) * 2 + lax.rem(low + b, 2) for a, b in turns]

    barrier = pltpu.get_barrier_semaphore()
    for k in range(1, n):
        pl.semaphore_signal(
            barrier, inc=1, device_id=(lax.rem(me + k, n), col), device_id_type=MESH
        )
    for peer in peers:
        pl.semaphore_signal(barrier, inc=1, device_id=(me, peer), device_id_type=MESH)
    pairs = (
        (features, feat),
        (hub_pick, pick),
        (halo_send, send),
        (w_self, weight.at[:, pl.ds(0, total_rows)]),
        (w_neigh, weight.at[:, pl.ds(total_rows, total_rows)]),
        (bias, bias_row),
        (tile_dst, dst),
        (tile_src, src),
        (tile_edges, edges),
        (tile_count, count_ref),
        (edge_src, esrc),
        (edge_dst, edst),
    )
    loads = [pltpu.make_async_copy(a, b, local_sem.at[i]) for i, (a, b) in enumerate(pairs)]
    for load in loads:
        load.start()
    running[0] = jnp.zeros_like(running[0])
    for load in loads[:3]:
        load.wait()
    for b in range(blocks):
        table[b] = feat[:, b * BLOCK : (b + 1) * BLOCK]
    for j in range(2 * halo):
        halo_buf[:, j * BLOCK : (j + 1) * BLOCK] = table[send[j]]
    for j in range(hub_per):
        hub_buf[:, j * BLOCK : (j + 1) * BLOCK] = table[pick[j]]
    hub_cols = hub_per * BLOCK
    halo_cols = halo * BLOCK
    own_hubs = pl.ds(pl.multiple_of(me * hub_cols, BLOCK), hub_cols)
    own_rows = pl.ds(pl.multiple_of(col * rows, rows), rows)
    own_nodes = pl.ds(pl.multiple_of(col * quarter, BLOCK), quarter)
    pl.semaphore_wait(barrier, n - 1 + f - 1)

    copies = []
    for side, peer in ((0, lax.rem(me + n - 1, n)), (1, lax.rem(me + 1, n))):
        start = n * hub_cols + (1 - side) * halo_cols
        copies.append(
            pltpu.make_async_remote_copy(
                src_ref=halo_buf.at[:, pl.ds(side * halo_cols, halo_cols)],
                dst_ref=ext.at[:, pl.ds(start, halo_cols)],
                send_sem=send_sem.at[n + side],
                recv_sem=recv_sem.at[n + side],
                device_id=(peer, col),
                device_id_type=MESH,
            )
        )
    for k in range(1, n):
        copies.append(
            pltpu.make_async_remote_copy(
                src_ref=hub_buf,
                dst_ref=ext.at[:, own_hubs],
                send_sem=send_sem.at[k],
                recv_sem=recv_sem.at[k],
                device_id=(lax.rem(me + k, n), col),
                device_id_type=MESH,
            )
        )
    for copy in copies:
        copy.start()
    feat_copies = []
    for k, peer in enumerate(peers):
        feat_copies.append(
            pltpu.make_async_remote_copy(
                src_ref=feat.at[:, pl.ds(pl.multiple_of(peer * quarter, BLOCK), quarter)],
                dst_ref=joined.at[own_rows, :],
                send_sem=feat_send.at[k],
                recv_sem=feat_recv.at[k],
                device_id=(me, peer),
                device_id_type=MESH,
            )
        )
    joined[own_rows, :] = feat[:, own_nodes]
    ext[:, own_hubs] = hub_buf[...]
    for load in loads[3:]:
        load.wait()

    count = count_ref[0]
    square = (BLOCK, BLOCK)
    lane = lax.broadcasted_iota(jnp.int32, square, 1).astype(jnp.float32)
    sub = lax.broadcasted_iota(jnp.int32, square, 0).astype(jnp.float32)
    spans = tiles // BLOCK
    tile = lax.broadcasted_iota(jnp.int32, square, 1)
    row = lax.broadcasted_iota(jnp.int32, square, 0)
    keys = [dst[i : i + 1, :] for i in range(spans)]
    best = [jnp.zeros((1, BLOCK), jnp.int32) for _ in range(spans + 1)]
    for i in range(spans):
        spread = jnp.transpose(jnp.broadcast_to(keys[i], square))
        place = row + (i * BLOCK + 1)
        for j in range(i, spans):
            found = spread == keys[j]
            if i == j:
                found = found & (row < tile)
            best[j] = jnp.maximum(
                best[j], jnp.max(jnp.where(found, place, 0), axis=0, keepdims=True)
            )
        best[spans] = jnp.maximum(
            best[spans], jnp.max(jnp.where(spread == tile, place, 0), axis=0, keepdims=True)
        )
    link_rows[...] = jnp.zeros_like(link_rows)
    for i in range(spans + 1):
        link_rows[i : i + 1, :] = best[i]
    link_load = pltpu.make_async_copy(link_rows, link, local_sem.at[12])
    link_load.start()
    for i in range(spans):
        order = lax.broadcasted_iota(jnp.int32, (1, BLOCK), 1) + i * BLOCK
        live = jnp.where(order < count, edges[i : i + 1, :], 0).astype(jnp.float32)
        target = jnp.transpose(edst[i * BLOCK : (i + 1) * BLOCK, :].astype(jnp.float32))
        target = jnp.where(sub < live, target, -1.0)
        for k in range(BLOCK // GROUP):
            columns[i * (BLOCK // GROUP) + k] = target[:, k * GROUP : (k + 1) * GROUP]

    def build(g, carry):
        for i in range(2):
            column = columns[g * 2 + i]
            for j in range(GROUP):
                match = jnp.broadcast_to(column[:, j : j + 1], square) == lane
                hot[(g * 2 + i) * GROUP + j] = jnp.where(match, 1.0, 0.0).astype(jnp.bfloat16)
        return carry

    lax.fori_loop(0, tiles // (2 * GROUP), build, 0)
    link_load.wait()
    for copy in feat_copies:
        copy.start()
    for copy in copies:
        copy.wait_recv()
    for b in range(ext.shape[1] // BLOCK):
        table[blocks + b] = ext[:, b * BLOCK : (b + 1) * BLOCK]
    ones = jnp.ones((16, BLOCK), jnp.bfloat16)

    def group(g, carry):
        first = pl.multiple_of(g * (STEP * GROUP), STEP * GROUP)
        parts = []
        for i in range(STEP):
            esrc_rows = esrc[pl.ds(first + i * GROUP, GROUP), :]
            for j in range(GROUP):
                t = first + i * GROUP + j
                values = table[src[t]]
                index = jnp.broadcast_to(esrc_rows[j : j + 1, :], values.shape).astype(jnp.int16)
                picked = lane_gather(values, index)
                left = jnp.concatenate([picked, ones], axis=0)
                part = jnp.dot(left, hot[t], preferred_element_type=jnp.float32)
                parts.append(part[: rows + 8])
        span = first // BLOCK
        spot = lax.rem(first, BLOCK)
        for j in range(STEP * GROUP):
            running[first + j + 1] = running[link[span, spot + j]] + parts[j]
        return carry

    lax.fori_loop(0, tiles // (STEP * GROUP), group, 0)

    width = quarter // CHUNKS
    per_chunk = width // BLOCK

    def chunk_means(owner, c):
        for i in range(per_chunk):
            b = owner * per_quarter + c * per_chunk + i
            total = running[link[spans, b]]
            degree = jnp.maximum(total[rows : rows + 1, :], 1.0)
            means[:, block_at(b)] = (total[:rows, :] / degree).astype(jnp.bfloat16)

    mean_rows = pl.ds(pl.multiple_of(total_rows + col * rows, rows), rows)
    mean_copies = []
    for c in range(CHUNKS):
        cols = pl.ds(c * width, width)
        for k, peer in enumerate(peers):
            chunk_means(peer, c)
            spot = pl.ds(pl.multiple_of(peer * quarter + c * width, BLOCK), width)
            mean_copies.append(
                pltpu.make_async_remote_copy(
                    src_ref=means.at[:, spot],
                    dst_ref=joined.at[mean_rows, cols],
                    send_sem=mean_send.at[c, k],
                    recv_sem=mean_recv.at[c, k],
                    device_id=(me, peer),
                    device_id_type=MESH,
                )
            )
            mean_copies[-1].start()
    for c in range(CHUNKS):
        chunk_means(col, c)
    joined[mean_rows, :] = means[:, own_nodes]
    column = jnp.transpose(jnp.broadcast_to(bias_row[...], (BLOCK, total_rows)))[:, :1]
    for copy in feat_copies:
        copy.wait_recv()
    out_copies = []
    own_copies = []
    for c in range(CHUNKS):
        cols = pl.ds(c * width, width)
        for copy in mean_copies[c * len(peers) : (c + 1) * len(peers)]:
            copy.wait_recv()
        total = jnp.dot(weight[...], joined[:, cols], preferred_element_type=jnp.float32)
        result[:, cols] = jnp.maximum(total + column, 0.0).astype(jnp.bfloat16)
        place = pl.ds(pl.multiple_of(col * quarter + c * width, BLOCK), width)
        for k, peer in enumerate(peers):
            out_copies.append(
                pltpu.make_async_remote_copy(
                    src_ref=result.at[pl.ds(pl.multiple_of(peer * rows, rows), rows), cols],
                    dst_ref=out.at[:, place],
                    send_sem=out_send.at[c, k],
                    recv_sem=out_recv.at[c, k],
                    device_id=(me, peer),
                    device_id_type=MESH,
                )
            )
            out_copies[-1].start()
        own_copies.append(
            pltpu.make_async_copy(
                result.at[own_rows, cols], out.at[:, place], own_sem.at[c]
            )
        )
        own_copies[-1].start()
    for copy in copies + feat_copies + mean_copies:
        copy.wait_send()
    for copy in out_copies + own_copies:
        copy.wait()


def shards(
    n,
    f,
    features,
    w_self,
    w_neigh,
    bias,
    hub_pick,
    halo_send,
    tile_dst,
    tile_src,
    tile_edges,
    tile_count,
    edge_src,
    edge_dst,
):
    rows, nodes = features.shape
    blocks = nodes // BLOCK
    tiles = tile_dst.shape[0]
    spans = tiles // BLOCK
    hub_per = hub_pick.shape[0]
    halo = halo_send.shape[0] // 2
    extra = n * hub_per + 2 * halo
    full = rows * f
    quarter = nodes // f
    bf16, f32, i32 = jnp.bfloat16, jnp.float32, jnp.int32
    vmem, smem, dma = pltpu.VMEM, pltpu.SMEM, pltpu.SemaphoreType.DMA
    return pl.pallas_call(
        functools.partial(layer_kernel, n, f),
        out_shape=vmem((rows, nodes), bf16),
        in_specs=[pl.BlockSpec(memory_space=pl.ANY)] * 12,
        out_specs=pl.BlockSpec(memory_space=pltpu.VMEM),
        scratch_shapes=[
            vmem((rows, nodes), bf16),
            vmem((full, 2 * full), bf16),
            vmem((1, full), f32),
            smem((hub_per,), i32),
            smem((2 * halo,), i32),
            vmem((spans, BLOCK), i32),
            smem((tiles,), i32),
            vmem((spans, BLOCK), i32),
            smem((1,), i32),
            vmem(edge_src.shape, i32),
            vmem(edge_dst.shape, i32),
            vmem((8, BLOCK), i32),
            smem((8, BLOCK), i32),
            vmem((tiles // GROUP, BLOCK, GROUP), f32),
            vmem((tiles, BLOCK, BLOCK), bf16),
            vmem((blocks + extra, rows, BLOCK), bf16),
            vmem((rows, hub_per * BLOCK), bf16),
            vmem((rows, 2 * halo * BLOCK), bf16),
            vmem((rows, extra * BLOCK), bf16),
            vmem((tiles + 1, rows + 8, BLOCK), f32),
            vmem((rows, nodes), bf16),
            vmem((2 * full, quarter), bf16),
            vmem((full, quarter), bf16),
            dma((13,)),
            dma((n + 2,)),
            dma((n + 2,)),
            dma((f,)),
            dma((f,)),
            dma((CHUNKS, f)),
            dma((CHUNKS, f)),
            dma((CHUNKS, f)),
            dma((CHUNKS, f)),
            dma((CHUNKS,)),
        ],
        compiler_params=pltpu.CompilerParams(
            collective_id=0, has_side_effects=True, vmem_limit_bytes=56 * 1024 * 1024
        ),
    )(
        features,
        w_self,
        w_neigh,
        bias.reshape(1, full),
        hub_pick,
        halo_send,
        tile_dst.reshape(spans, BLOCK),
        tile_src,
        tile_edges.reshape(spans, BLOCK),
        tile_count,
        edge_src,
        edge_dst,
    )


def solution(mesh):
    in_specs = (
        P("feat", "graph"),
        P(),
        P(),
        P(),
        P("graph"),
        P("graph"),
        P("graph"),
        P("graph"),
        P("graph"),
        P("graph"),
        P("graph", None),
        P("graph", None),
    )
    return jax.shard_map(
        functools.partial(shards, mesh.shape["graph"], mesh.shape["feat"]),
        mesh=mesh,
        in_specs=in_specs,
        out_specs=P("feat", "graph"),
        check_vma=False,
    )
```
